512 devices in a mesh: dp: 2 (over y_lo), ctx: 64 (over z, y_hi, core), tp: 4 (over x).
Axes of the slice: x: 4, y: 4 (y_hi: 2, y_lo: 2; y = y_hi * 2 + y_lo), z: 16, core: 2. Of those that a mesh axis runs over, the one named last changes fastest.
Arguments:
- values: bfloat16 [2, 8192, 4096], P('dp', 'ctx', 'tp'), may hold values from -6 to 6
- gate_input: bfloat16 [2, 8192, 4096], P('dp', 'ctx', 'tp'), may hold values from -6 to 6
- filter_param: bfloat16 [8192, 4096], P('ctx', 'tp'), may hold values from -6 to 6
- grad_y: bfloat16 [2, 8192, 4096], P('dp', 'ctx', 'tp'), may hold values from -6 to 6
Outputs:
- grad_gate: bfloat16 [2, 8192, 4096], P('dp', 'ctx', 'tp')
- grad_values: bfloat16 [2, 8192, 4096], P('dp', 'ctx', 'tp')
- grad_filter: float32 [8192, 4096], P('ctx', 'tp')
The draws below stay inside these ranges and needn't reach their ends.
All inputs are finite; a program needn't handle non-finite values.
Results may differ from the reference program's by a relative error of at most 0.01.
Values may be sent and summed in bfloat16 or wider, within the bound.
A program may use at most 64 MiB of HBM per device.

```python
import math
import jax
import jax.numpy as jnp
from jax import lax

C = 4096
SEQS = 2
LENGTH = 8192


def block_levels(own_key, extent, pieces, least, largest):
    loudness = 1.0
    for position, blocks in pieces:
        heights = jax.random.uniform(jax.random.fold_in(jax.random.fold_in(own_key, 6), position), (blocks,), jnp.float32, least / len(pieces), largest / len(pieces))
        loudness = loudness * jnp.repeat(jnp.exp(heights), extent[position] // blocks).reshape((-1,) + (1,) * (len(extent) - 1 - position))
    return loudness


def normal_values(key, dims, spread, bound, cuts=(), kind=jnp.bfloat16):
    result = spread * jax.random.normal(key, dims, jnp.float32)
    if cuts:
        result = result * block_levels(key, dims, cuts, -0.22, 0.18)
    return jnp.clip(result, -bound, bound).astype(kind)


def setup_inputs(seed: int = 0) -> dict:
    key_of = jax.random.split(jax.random.key(seed), 5)
    return {
        "values": normal_values(key_of[0], (SEQS, LENGTH, C), 1.0, 6.0, ((0, 2), (1, 64), (2, 4))),
        "gate_input": normal_values(key_of[1], (SEQS, LENGTH, C), 1.0, 6.0, ((0, 2), (1, 64), (2, 4))),
        "filter_param": normal_values(key_of[2], (LENGTH, C), 1.0, 6.0, ((0, 64), (1, 4))),
        "grad_y": normal_values(key_of[3], (SEQS, LENGTH, C), 1.0, 6.0, ((0, 2), (1, 64), (2, 4))),
    }


def block_grads(blocks):
    values, gate_input, filter_param, grad_y = blocks
    length = values.shape[1]
    padded = 2 * length
    inv_root = 1.0 / math.sqrt(length)
    grad_rows = grad_y.astype(jnp.float32)
    grad_s = (grad_rows * gate_input.astype(jnp.float32)).astype(jnp.bfloat16)
    val_spec = jnp.fft.rfft(values.astype(jnp.float32), n=padded, axis=1)
    filt_spec = jnp.fft.rfft(filter_param.astype(jnp.float32), n=padded, axis=0) * inv_root
    grad_spec = jnp.fft.rfft(grad_s.astype(jnp.float32), n=padded, axis=1)
    conv_out = jnp.fft.irfft(val_spec * filt_spec[None], n=padded, axis=1)[:, :length]
    grad_gate = (grad_rows * conv_out).astype(jnp.bfloat16)
    grad_values = jnp.fft.irfft(grad_spec * jnp.conj(filt_spec)[None], n=padded, axis=1)[:, :length]
    cross_spec = lax.optimization_barrier(jnp.sum(grad_spec * jnp.conj(val_spec), axis=0))
    grad_filter = jnp.fft.irfft(cross_spec, n=padded, axis=0)[:length] * inv_root
    return (grad_gate, grad_values.astype(jnp.bfloat16), grad_filter.astype(jnp.float32))

def reference(values, gate_input, filter_param, grad_y):
    seqs, length, chans = values.shape
    width = min(chans, 512)
    count = chans // width

    def split_seq(array):
        return jnp.transpose(array.reshape(seqs, length, count, width), (2, 0, 1, 3))
    filt_blocks = jnp.transpose(filter_param.reshape(length, count, width), (1, 0, 2))
    gate_b, vals_b, filt_b = lax.map(block_grads, (split_seq(values), split_seq(gate_input), filt_blocks, split_seq(grad_y)))

    def join_seq(array):
        return jnp.transpose(array, (1, 2, 0, 3)).reshape(seqs, length, chans)
    grad_filter = jnp.transpose(filt_b, (1, 0, 2)).reshape(length, chans)
    return (join_seq(gate_b), join_seq(vals_b), grad_filter)
```

```python
import functools
import math

import jax
import jax.numpy as jnp
import numpy as np
from jax import lax
from jax.experimental import pallas as pl
from jax.experimental.pallas import tpu as pltpu
from jax.sharding import PartitionSpec as P

MESH = pl.DeviceIdType.MESH
F32 = jnp.float32
BF16 = jnp.bfloat16
LANES = 128
GROUP = 4


def make_tables(blocks, width):
    length = blocks * width
    half = blocks // 2
    block_of = np.concatenate([np.arange(half) * 2, np.arange(half) * 2 + 1]).astype(np.float64)
    k1 = np.arange(blocks, dtype=np.float64) + 0.25
    n2 = np.arange(width, dtype=np.float64)
    ang1 = 2.0 * np.pi * k1[:, None] * block_of[None, :] / blocks
    d1 = np.concatenate([np.cos(ang1), -np.sin(ang1)], axis=0)
    d4 = np.concatenate([np.cos(ang1), -np.sin(ang1)], axis=0).T
    ang2 = 2.0 * np.pi * k1[:, None] * n2[None, :] / length
    tw = np.concatenate([np.cos(ang2), np.sin(ang2)], axis=1)
    scale = 1.0 / (length * math.sqrt(length))
    ang3 = 2.0 * np.pi * n2[:, None] * n2[None, :] / width
    co, si = np.cos(ang3), np.sin(ang3)
    fwd = np.block([[co, -si], [si, co]])
    inv = np.block([[co, si], [-si, co]])
    return (
        jnp.asarray(d1, BF16),
        jnp.asarray(d4, BF16),
        jnp.asarray(np.concatenate([tw, tw * scale], axis=1), F32),
        jnp.asarray(fwd, BF16),
        jnp.asarray(inv, BF16),
    )


def kernel(
    blocks,
    v_hbm, gate_hbm, f_hbm, gy_hbm, d1_hbm, d4_hbm, tw_hbm, fwd_hbm, inv_hbm,
    gg_hbm, gv_hbm, gf_hbm,
    in_v, in_gate, in_f, in_gy, d1, d4, tw, fwd, inv,
    s_h, s_v, s_g, r_h, r_v, r_g,
    x32, y32, spec_h, spec_v, spec_g,
    s_c, s_gv, s_gf, r_pair, r_c, r_gv, r_gf,
    o_gg, o_gv, o_gf,
    in_sem, send_sem, recv_sem, out_sem,
):
    chans = in_v.shape[1]
    width = in_v.shape[0]
    ch = chans // blocks
    half = blocks // 2
    rows_half = half * ch
    d = lax.axis_index("dp")
    q = lax.axis_index("ctx")
    core = q % 2
    my_z, my_e = q // 4, q % 4
    zs = blocks // 4
    my_slot = core * half + q // 2

    loads = [
        pltpu.make_async_copy(src, dst, in_sem.at[i])
        for i, (src, dst) in enumerate(
            [
                (f_hbm, in_f), (v_hbm.at[0], in_v), (gy_hbm.at[0], in_gy), (gate_hbm.at[0], in_gate),
                (d1_hbm, d1), (tw_hbm, tw), (fwd_hbm, fwd), (inv_hbm, inv), (d4_hbm, d4),
            ]
        )
    ]
    for load in loads:
        load.start()

    def peer(k):
        step, e = k // 4, k % 4
        dist = (step + 1) // 2
        dz = jnp.where(step % 2 == 1, dist, zs - dist)
        return ((my_z + dz) % zs) * 4 + (my_e + e) % 4

    barrier = pltpu.get_barrier_semaphore()

    def greet(k, carry):
        pl.semaphore_signal(barrier, inc=1, device_id={"ctx": peer(k)}, device_id_type=MESH)
        return carry

    lax.fori_loop(1, blocks, greet, 0)
    pl.semaphore_signal(barrier, inc=1, device_id={"dp": 1 - d}, device_id_type=MESH)

    def rows(ref, start, count):
        return ref.at[pl.ds(pl.multiple_of(start, 16), count), :]

    def wait_bytes(ref, sem):
        pltpu.make_async_copy(ref, ref, sem).wait()

    def transpose_in(block_of, dst):
        for j in range(chans // LANES):
            dst[j * LANES:(j + 1) * LANES, :] = block_of(slice(j * LANES, (j + 1) * LANES)).T.astype(BF16)

    def send_in(src, dst, sem):
        pltpu.make_async_copy(rows(src, q * ch, ch), rows(dst, my_slot * ch, ch), recv_sem.at[sem]).start()

        def one(k, carry):
            to = peer(k)
            pltpu.make_async_remote_copy(
                src_ref=rows(src, to * ch, ch), dst_ref=rows(dst, my_slot * ch, ch),
                send_sem=send_sem.at[sem], recv_sem=recv_sem.at[sem],
                device_id={"ctx": to}, device_id_type=MESH,
            ).start()
            return carry

        lax.fori_loop(1, blocks, one, 0)

    def send_out(src, dst, sem):
        pltpu.make_async_copy(rows(src, my_slot * ch, ch), rows(dst, q * ch, ch), recv_sem.at[sem]).start()

        def one(k, carry):
            to = peer(k)
            slot = (to % 2) * half + to // 2
            pltpu.make_async_remote_copy(
                src_ref=rows(src, slot * ch, ch), dst_ref=rows(dst, q * ch, ch),
                send_sem=send_sem.at[sem], recv_sem=recv_sem.at[sem],
                device_id={"ctx": to}, device_id_type=MESH,
            ).start()
            return carry

        lax.fori_loop(1, blocks, one, 0)

    def pair_copy(src, dst, sem):
        return pltpu.make_async_remote_copy(
            src_ref=src, dst_ref=dst, send_sem=send_sem.at[sem], recv_sem=recv_sem.at[sem],
            device_id={"dp": 1 - d}, device_id_type=MESH,
        )

    H, V, G, HP, CO, GV, GP, GF, GFP = range(9)

    loads[0].wait()
    transpose_in(lambda s: in_f[:, s].astype(F32), s_h)
    pl.semaphore_wait(barrier, blocks)

    @pl.when(core == d)
    def _():
        send_in(s_h, r_h, H)

    loads[1].wait()
    transpose_in(lambda s: in_v[:, s].astype(F32), s_v)
    send_in(s_v, r_v, V)
    loads[2].wait()
    loads[3].wait()
    transpose_in(lambda s: (in_gy[:, s].astype(F32) * in_gate[:, s].astype(F32)).astype(BF16).astype(F32), s_g)
    send_in(s_g, r_g, G)
    for load in loads[4:]:
        load.wait()

    def tw_at(i):
        return tw[:, i * LANES:(i + 1) * LANES]

    def forward(src, spec):
        x32[...] = src[...].astype(F32)
        for g in range(0, ch, GROUP):
            x = jnp.concatenate(
                [x32[pl.ds(c, blocks, stride=ch), :].astype(BF16) for c in range(g, g + GROUP)], axis=1
            )
            a = jnp.dot(d1[...], x, preferred_element_type=F32)
            turned = []
            for c in range(GROUP):
                re = a[:blocks, c * LANES:(c + 1) * LANES]
                im = a[blocks:, c * LANES:(c + 1) * LANES]
                turned.append(
                    jnp.concatenate(
                        [
                            (re * tw_at(0) + im * tw_at(1)).astype(BF16),
                            (im * tw_at(0) - re * tw_at(1)).astype(BF16),
                        ],
                        axis=1,
                    )
                )
            spec[g * blocks:(g + GROUP) * blocks, :] = jnp.dot(
                jnp.concatenate(turned, axis=0), fwd[...], preferred_element_type=F32
            )

    def inverse(left, right, sign, dst):
        for g in range(0, ch, GROUP):
            part = slice(g * blocks, (g + GROUP) * blocks)
            lr, li = left[part, :LANES], left[part, LANES:]
            rr, ri = right[part, :LANES], right[part, LANES:]
            if sign > 0:
                pr, pi = lr * rr - li * ri, lr * ri + li * rr
            else:
                pr, pi = lr * rr + li * ri, li * rr - lr * ri
            prod = jnp.concatenate([pr.astype(BF16), pi.astype(BF16)], axis=1)
            b = jnp.dot(prod, inv[...], preferred_element_type=F32)
            turned = []
            for c in range(GROUP):
                re = b[c * blocks:(c + 1) * blocks, :LANES]
                im = b[c * blocks:(c + 1) * blocks, LANES:]
                turned.append(
                    jnp.concatenate(
                        [
                            (re * tw_at(2) - im * tw_at(3)).astype(BF16),
                            (im * tw_at(2) + re * tw_at(3)).astype(BF16),
                        ],
                        axis=0,
                    )
                )
            y = jnp.dot(d4[...], jnp.concatenate(turned, axis=1), preferred_element_type=F32)
            for c in range(GROUP):
                y32[pl.ds(g + c, blocks, stride=ch), :] = y[:, c * LANES:(c + 1) * LANES]
        dst[...] = y32[...].astype(BF16)

    straight = rows(r_h, d * rows_half, rows_half)
    wait_bytes(straight, recv_sem.at[H])
    filter_pass = pair_copy(straight, straight, HP)
    filter_pass.start()
    wait_bytes(r_v, recv_sem.at[V])
    forward(r_v, spec_v)
    filter_pass.wait()
    forward(r_h, spec_h)
    inverse(spec_v, spec_h, 1, s_c)
    send_out(s_c, r_c, CO)

    wait_bytes(r_g, recv_sem.at[G])
    forward(r_g, spec_g)
    inverse(spec_g, spec_v, -1, s_gf)
    mine = rows(s_gf, d * rows_half, rows_half)
    grad_pass = pair_copy(rows(s_gf, (1 - d) * rows_half, rows_half), r_pair, GP)
    grad_pass.start()
    inverse(spec_g, spec_h, -1, s_gv)
    send_out(s_gv, r_gv, GV)
    grad_pass.wait()
    at = pl.ds(pl.multiple_of(d * rows_half, 16), rows_half)
    s_gf[at, :] = (s_gf[at, :].astype(F32) + r_pair[...].astype(F32)).astype(BF16)

    def send_grad(k, carry):
        slot = d * half + (my_slot + k) % half
        to = ((my_slot + k) % half) * 2 + d

        @pl.when(to != q)
        def _():
            pltpu.make_async_remote_copy(
                src_ref=rows(s_gf, slot * ch, ch), dst_ref=rows(r_gf, q * ch, ch),
                send_sem=send_sem.at[GF], recv_sem=recv_sem.at[GF],
                device_id={"ctx": to}, device_id_type=MESH,
            ).start()

        return carry

    lax.fori_loop(0, half, send_grad, 0)

    @pl.when(core == d)
    def _():
        pltpu.make_async_copy(rows(s_gf, my_slot * ch, ch), rows(r_gf, q * ch, ch), recv_sem.at[GF]).start()

    wait_bytes(r_c, recv_sem.at[CO])
    for j in range(chans // LANES):
        s = slice(j * LANES, (j + 1) * LANES)
        o_gg[:, s] = (in_gy[:, s].astype(F32) * r_c[s, :].astype(F32).T).astype(BF16)
    out_gg = pltpu.make_async_copy(o_gg, gg_hbm.at[0], out_sem.at[0])
    out_gg.start()

    wait_bytes(r_gv, recv_sem.at[GV])
    for j in range(chans // LANES):
        s = slice(j * LANES, (j + 1) * LANES)
        o_gv[:, s] = r_gv[s, :].astype(F32).T.astype(BF16)
    out_gv = pltpu.make_async_copy(o_gv, gv_hbm.at[0], out_sem.at[1])
    out_gv.start()

    wait_bytes(r_gf, recv_sem.at[GF])

    @pl.when(core == d)
    def _():
        last = pair_copy(r_gf, r_gf, GF)
        last.start()

    for j in range(chans // LANES):
        s = slice(j * LANES, (j + 1) * LANES)
        o_gf[:, s] = r_gf[s, :].astype(F32).T
    out_gf = pltpu.make_async_copy(o_gf, gf_hbm, out_sem.at[2])
    out_gf.start()

    most = (blocks - 1) * ch

    @pl.when(core == d)
    def _():
        wait_bytes(s_h.at[pl.ds(0, most), :], send_sem.at[H])
        wait_bytes(s_gf.at[pl.ds(0, rows_half - ch), :], send_sem.at[GF])
        wait_bytes(r_gf, send_sem.at[GF])

    @pl.when(core != d)
    def _():
        wait_bytes(s_gf.at[pl.ds(0, rows_half), :], send_sem.at[GF])

    for ref, sem in ((s_v, V), (s_g, G), (s_c, CO), (s_gv, GV)):
        wait_bytes(ref.at[pl.ds(0, most), :], send_sem.at[sem])
    out_gg.wait()
    out_gv.wait()
    out_gf.wait()


def body(values, gate_input, filter_param, grad_y, *tables):
    blocks = lax.axis_size("ctx")
    width, chans = filter_param.shape
    vm = lambda shape, kind: pltpu.VMEM(shape, kind)
    block = (width, chans)
    tiles = (chans, width)
    spec = (chans, 2 * width)
    any_spec = pl.BlockSpec(memory_space=pl.ANY)
    return pl.pallas_call(
        functools.partial(kernel, blocks),
        out_shape=(
            jax.ShapeDtypeStruct((1, width, chans), BF16),
            jax.ShapeDtypeStruct((1, width, chans), BF16),
            jax.ShapeDtypeStruct((width, chans), F32),
        ),
        in_specs=[any_spec] * 9,
        out_specs=(any_spec,) * 3,
        scratch_shapes=[vm(block, BF16)] * 4
        + [vm(t.shape, t.dtype) for t in tables]
        + [vm(tiles, BF16)] * 6
        + [vm(tiles, F32)] * 2
        + [vm(spec, F32)] * 3
        + [vm(tiles, BF16)] * 3
        + [vm((chans // 2, width), BF16)]
        + [vm(tiles, BF16)] * 3
        + [vm(block, BF16)] * 2
        + [vm(block, F32)]
        + [
            pltpu.SemaphoreType.DMA((9,)),
            pltpu.SemaphoreType.DMA((9,)),
            pltpu.SemaphoreType.DMA((9,)),
            pltpu.SemaphoreType.DMA((3,)),
        ],
        compiler_params=pltpu.CompilerParams(
            collective_id=0, has_side_effects=True, vmem_limit_bytes=40 * 1024 * 1024
        ),
        cost_estimate=pl.CostEstimate(flops=1_000_000_000, bytes_accessed=4_000_000, transcendentals=0),
    )(values, gate_input, filter_param, grad_y, *tables)


def solution(mesh):
    blocks = mesh.shape["ctx"]
    tables = make_tables(blocks, LANES)
    placed = (P("dp", "ctx", "tp"), P("dp", "ctx", "tp"), P("ctx", "tp"), P("dp", "ctx", "tp"))
    mapped = jax.shard_map(
        body,
        mesh=mesh,
        in_specs=placed + (P(),) * len(tables),
        out_specs=(P("dp", "ctx", "tp"), P("dp", "ctx", "tp"), P("ctx", "tp")),
        check_vma=False,
    )

    def run(values, gate_input, filter_param, grad_y):
        return mapped(values, gate_input, filter_param, grad_y, *tables)

    return run
```

```python
import functools
import math

import jax
import jax.numpy as jnp
import numpy as np
from jax import lax
from jax.experimental import pallas as pl
from jax.experimental.pallas import tpu as pltpu
from jax.sharding import PartitionSpec as P

MESH = pl.DeviceIdType.MESH
F32 = jnp.float32
BF16 = jnp.bfloat16
LANES = 128
GROUP = 4


def make_tables(blocks, width):
    length = blocks * width
    half = blocks // 2
    block_of = np.concatenate([np.arange(half) * 2, np.arange(half) * 2 + 1]).astype(np.float64)
    k1 = np.arange(blocks, dtype=np.float64) + 0.25
    n2 = np.arange(width, dtype=np.float64)
    ang1 = 2.0 * np.pi * k1[:, None] * block_of[None, :] / blocks
    d1 = np.concatenate([np.cos(ang1), -np.sin(ang1)], axis=0)
    d4 = np.concatenate([np.cos(ang1), -np.sin(ang1)], axis=0).T
    ang2 = 2.0 * np.pi * k1[:, None] * n2[None, :] / length
    tw = np.concatenate([np.cos(ang2), np.sin(ang2)], axis=1)
    scale = 1.0 / (length * math.sqrt(length))
    ang3 = 2.0 * np.pi * n2[:, None] * n2[None, :] / width
    co, si = np.cos(ang3), np.sin(ang3)
    fwd = np.block([[co, -si], [si, co]])
    inv = np.block([[co, si], [-si, co]])
    return (
        jnp.asarray(d1, BF16),
        jnp.asarray(d4, BF16),
        jnp.asarray(np.concatenate([tw, tw * scale], axis=1), F32),
        jnp.asarray(fwd, BF16),
        jnp.asarray(inv, BF16),
    )


def kernel(
    blocks,
    v_hbm, gate_hbm, f_hbm, gy_hbm, d1_hbm, d4_hbm, tw_hbm, fwd_hbm, inv_hbm,
    gg_hbm, gv_hbm, gf_hbm,
    in_v, in_gate, in_f, in_gy, d1, d4, tw, fwd, inv,
    s_h, s_v, s_g, r_h, r_v, r_g,
    x32, y32, spec_h, spec_v, spec_g,
    s_c, s_gv, s_gf, r_pair, r_c, r_gv, r_gf,
    o_gg, o_gv, o_gf,
    in_sem, send_sem, recv_sem, out_sem,
):
    chans = in_v.shape[1]
    width = in_v.shape[0]
    ch = chans // blocks
    half = blocks // 2
    rows_half = half * ch
    d = lax.axis_index("dp")
    q = lax.axis_index("ctx")
    core = q % 2
    my_z, my_e = q // 4, q % 4
    zs = blocks // 4
    my_slot = core * half + q // 2

    loads = [
        pltpu.make_async_copy(src, dst, in_sem.at[i])
        for i, (src, dst) in enumerate(
            [
                (f_hbm, in_f), (v_hbm.at[0], in_v), (gy_hbm.at[0], in_gy), (gate_hbm.at[0], in_gate),
                (d1_hbm, d1), (tw_hbm, tw), (fwd_hbm, fwd), (inv_hbm, inv), (d4_hbm, d4),
            ]
        )
    ]
    for load in loads:
        load.start()

    def peer(k):
        step, e = k // 4, k % 4
        turn = step // 2
        dist = (turn + 1) // 2
        dz = jnp.where(turn % 2 == 1, zs - dist, dist) + (step % 2) * (zs // 2)
        return ((my_z + dz) % zs) * 4 + (my_e + e) % 4

    barrier = pltpu.get_barrier_semaphore()

    def greet(k, carry):
        pl.semaphore_signal(barrier, inc=1, device_id={"ctx": peer(k)}, device_id_type=MESH)
        return carry

    lax.fori_loop(1, blocks, greet, 0)
    pl.semaphore_signal(barrier, inc=1, device_id={"dp": 1 - d}, device_id_type=MESH)

    def rows(ref, start, count):
        return ref.at[pl.ds(pl.multiple_of(start, 16), count), :]

    def wait_bytes(ref, sem):
        pltpu.make_async_copy(ref, ref, sem).wait()

    def transpose_in(block_of, dst):
        for j in range(chans // LANES):
            dst[j * LANES:(j + 1) * LANES, :] = block_of(slice(j * LANES, (j + 1) * LANES)).T.astype(BF16)

    def send_in(src, dst, sem):
        pltpu.make_async_copy(rows(src, q * ch, ch), rows(dst, my_slot * ch, ch), recv_sem.at[sem]).start()

        def one(k, carry):
            to = peer(k)
            pltpu.make_async_remote_copy(
                src_ref=rows(src, to * ch, ch), dst_ref=rows(dst, my_slot * ch, ch),
                send_sem=send_sem.at[sem], recv_sem=recv_sem.at[sem],
                device_id={"ctx": to}, device_id_type=MESH,
            ).start()
            return carry

        lax.fori_loop(1, blocks, one, 0)

    def send_out(src, dst, sem, first=0, last=blocks):
        if first == 0:
            pltpu.make_async_copy(rows(src, my_slot * ch, ch), rows(dst, q * ch, ch), recv_sem.at[sem]).start()

        def one(k, carry):
            to = peer(k)
            slot = (to % 2) * half + to // 2
            pltpu.make_async_remote_copy(
                src_ref=rows(src, slot * ch, ch), dst_ref=rows(dst, q * ch, ch),
                send_sem=send_sem.at[sem], recv_sem=recv_sem.at[sem],
                device_id={"ctx": to}, device_id_type=MESH,
            ).start()
            return carry

        lax.fori_loop(max(first, 1), last, one, 0)

    def pair_copy(src, dst, sem):
        return pltpu.make_async_remote_copy(
            src_ref=src, dst_ref=dst, send_sem=send_sem.at[sem], recv_sem=recv_sem.at[sem],
            device_id={"dp": 1 - d}, device_id_type=MESH,
        )

    H, V, G, HP, CO, GV, GP, GF, GFP = range(9)

    loads[0].wait()
    transpose_in(lambda s: in_f[:, s].astype(F32), s_h)
    pl.semaphore_wait(barrier, blocks)

    @pl.when(core == d)
    def _():
        send_in(s_h, r_h, H)

    loads[1].wait()
    transpose_in(lambda s: in_v[:, s].astype(F32), s_v)
    send_in(s_v, r_v, V)
    loads[2].wait()
    loads[3].wait()
    transpose_in(lambda s: (in_gy[:, s].astype(F32) * in_gate[:, s].astype(F32)).astype(BF16).astype(F32), s_g)
    for load in loads[4:]:
        load.wait()

    def tw_at(i):
        return tw[:, i * LANES:(i + 1) * LANES]

    def forward(src, spec):
        x32[...] = src[...].astype(F32)
        for g in range(0, ch, GROUP):
            x = jnp.concatenate(
                [x32[pl.ds(c, blocks, stride=ch), :].astype(BF16) for c in range(g, g + GROUP)], axis=1
            )
            a = jnp.dot(d1[...], x, preferred_element_type=F32)
            turned = []
            for c in range(GROUP):
                re = a[:blocks, c * LANES:(c + 1) * LANES]
                im = a[blocks:, c * LANES:(c + 1) * LANES]
                turned.append(
                    jnp.concatenate(
                        [
                            (re * tw_at(0) + im * tw_at(1)).astype(BF16),
                            (im * tw_at(0) - re * tw_at(1)).astype(BF16),
                        ],
                        axis=1,
                    )
                )
            spec[g * blocks:(g + GROUP) * blocks, :] = jnp.dot(
                jnp.concatenate(turned, axis=0), fwd[...], preferred_element_type=F32
            )

    def inverse(left, right, sign, dst):
        for g in range(0, ch, GROUP):
            part = slice(g * blocks, (g + GROUP) * blocks)
            lr, li = left[part, :LANES], left[part, LANES:]
            rr, ri = right[part, :LANES], right[part, LANES:]
            if sign > 0:
                pr, pi = lr * rr - li * ri, lr * ri + li * rr
            else:
                pr, pi = lr * rr + li * ri, li * rr - lr * ri
            prod = jnp.concatenate([pr.astype(BF16), pi.astype(BF16)], axis=1)
            b = jnp.dot(prod, inv[...], preferred_element_type=F32)
            turned = []
            for c in range(GROUP):
                re = b[c * blocks:(c + 1) * blocks, :LANES]
                im = b[c * blocks:(c + 1) * blocks, LANES:]
                turned.append(
                    jnp.concatenate(
                        [
                            (re * tw_at(2) - im * tw_at(3)).astype(BF16),
                            (im * tw_at(2) + re * tw_at(3)).astype(BF16),
                        ],
                        axis=0,
                    )
                )
            y = jnp.dot(d4[...], jnp.concatenate(turned, axis=1), preferred_element_type=F32)
            for c in range(GROUP):
                y32[pl.ds(g + c, blocks, stride=ch), :] = y[:, c * LANES:(c + 1) * LANES]
        dst[...] = y32[...].astype(BF16)

    straight = rows(r_h, d * rows_half, rows_half)
    wait_bytes(straight, recv_sem.at[H])
    filter_pass = pair_copy(straight, straight, HP)
    filter_pass.start()
    send_in(s_g, r_g, G)
    wait_bytes(r_v, recv_sem.at[V])
    forward(r_v, spec_v)
    filter_pass.wait()
    forward(r_h, spec_h)
    inverse(spec_v, spec_h, 1, s_c)
    send_out(s_c, r_c, CO)

    wait_bytes(r_g, recv_sem.at[G])
    forward(r_g, spec_g)
    inverse(spec_g, spec_v, -1, s_gf)
    mine = rows(s_gf, d * rows_half, rows_half)
    grad_pass = pair_copy(rows(s_gf, (1 - d) * rows_half, rows_half), r_pair, GP)
    grad_pass.start()
    inverse(spec_g, spec_h, -1, s_gv)
    send_out(s_gv, r_gv, GV, 0, half)
    grad_pass.wait()
    at = pl.ds(pl.multiple_of(d * rows_half, 16), rows_half)
    s_gf[at, :] = (s_gf[at, :].astype(F32) + r_pair[...].astype(F32)).astype(BF16)

    def send_grad(k, carry):
        to = peer((k // 2) * 4 + (k % 2) * 2 + (core + d) % 2)
        slot = d * half + to // 2

        @pl.when(to != q)
        def _():
            pltpu.make_async_remote_copy(
                src_ref=rows(s_gf, slot * ch, ch), dst_ref=rows(r_gf, q * ch, ch),
                send_sem=send_sem.at[GF], recv_sem=recv_sem.at[GF],
                device_id={"ctx": to}, device_id_type=MESH,
            ).start()

        return carry

    lax.fori_loop(0, half, send_grad, 0)

    @pl.when(core == d)
    def _():
        pltpu.make_async_copy(rows(s_gf, my_slot * ch, ch), rows(r_gf, q * ch, ch), recv_sem.at[GF]).start()

    send_out(s_gv, r_gv, GV, half, blocks)

    wait_bytes(r_c, recv_sem.at[CO])
    for j in range(chans // LANES):
        s = slice(j * LANES, (j + 1) * LANES)
        o_gg[:, s] = (in_gy[:, s].astype(F32) * r_c[s, :].astype(F32).T).astype(BF16)
    out_gg = pltpu.make_async_copy(o_gg, gg_hbm.at[0], out_sem.at[0])
    out_gg.start()

    out_gf = pltpu.make_async_copy(o_gf, gf_hbm, out_sem.at[2])

    def give_gf():
        for j in range(chans // LANES):
            s = slice(j * LANES, (j + 1) * LANES)
            o_gf[:, s] = r_gf[s, :].astype(F32).T
        out_gf.start()

    @pl.when(core == d)
    def _():
        wait_bytes(r_gf, recv_sem.at[GF])
        pair_copy(r_gf, r_gf, GF).start()
        give_gf()

    wait_bytes(r_gv, recv_sem.at[GV])
    for j in range(chans // LANES):
        s = slice(j * LANES, (j + 1) * LANES)
        o_gv[:, s] = r_gv[s, :].astype(F32).T.astype(BF16)
    out_gv = pltpu.make_async_copy(o_gv, gv_hbm.at[0], out_sem.at[1])
    out_gv.start()

    @pl.when(core != d)
    def _():
        wait_bytes(r_gf, recv_sem.at[GF])
        give_gf()

    most = (blocks - 1) * ch

    @pl.when(core == d)
    def _():
        wait_bytes(s_h.at[pl.ds(0, most), :], send_sem.at[H])
        wait_bytes(s_gf.at[pl.ds(0, rows_half - ch), :], send_sem.at[GF])
        wait_bytes(r_gf, send_sem.at[GF])

    @pl.when(core != d)
    def _():
        wait_bytes(s_gf.at[pl.ds(0, rows_half), :], send_sem.at[GF])

    for ref, sem in ((s_v, V), (s_g, G), (s_c, CO), (s_gv, GV)):
        wait_bytes(ref.at[pl.ds(0, most), :], send_sem.at[sem])
    out_gg.wait()
    out_gv.wait()
    out_gf.wait()


def body(values, gate_input, filter_param, grad_y, *tables):
    blocks = lax.axis_size("ctx")
    width, chans = filter_param.shape
    vm = lambda shape, kind: pltpu.VMEM(shape, kind)
    block = (width, chans)
    tiles = (chans, width)
    spec = (chans, 2 * width)
    any_spec = pl.BlockSpec(memory_space=pl.ANY)
    return pl.pallas_call(
        functools.partial(kernel, blocks),
        out_shape=(
            jax.ShapeDtypeStruct((1, width, chans), BF16),
            jax.ShapeDtypeStruct((1, width, chans), BF16),
            jax.ShapeDtypeStruct((width, chans), F32),
        ),
        in_specs=[any_spec] * 9,
        out_specs=(any_spec,) * 3,
        scratch_shapes=[vm(block, BF16)] * 4
        + [vm(t.shape, t.dtype) for t in tables]
        + [vm(tiles, BF16)] * 6
        + [vm(tiles, F32)] * 2
        + [vm(spec, F32)] * 3
        + [vm(tiles, BF16)] * 3
        + [vm((chans // 2, width), BF16)]
        + [vm(tiles, BF16)] * 3
        + [vm(block, BF16)] * 2
        + [vm(block, F32)]
        + [
            pltpu.SemaphoreType.DMA((9,)),
            pltpu.SemaphoreType.DMA((9,)),
            pltpu.SemaphoreType.DMA((9,)),
            pltpu.SemaphoreType.DMA((3,)),
        ],
        compiler_params=pltpu.CompilerParams(
            collective_id=0, has_side_effects=True, vmem_limit_bytes=64 * 1024 * 1024
        ),
        cost_estimate=pl.CostEstimate(flops=1_000_000_000, bytes_accessed=4_000_000, transcendentals=0),
    )(values, gate_input, filter_param, grad_y, *tables)


def solution(mesh):
    blocks = mesh.shape["ctx"]
    tables = make_tables(blocks, LANES)
    placed = (P("dp", "ctx", "tp"), P("dp", "ctx", "tp"), P("ctx", "tp"), P("dp", "ctx", "tp"))
    mapped = jax.shard_map(
        body,
        mesh=mesh,
        in_specs=placed + (P(),) * len(tables),
        out_specs=(P("dp", "ctx", "tp"), P("dp", "ctx", "tp"), P("ctx", "tp")),
        check_vma=False,
    )

    def run(values, gate_input, filter_param, grad_y):
        return mapped(values, gate_input, filter_param, grad_y, *tables)

    return run
```

```python
import functools
import math

import jax
import jax.numpy as jnp
import numpy as np
from jax import lax
from jax.experimental import pallas as pl
from jax.experimental.pallas import tpu as pltpu
from jax.sharding import PartitionSpec as P

MESH = pl.DeviceIdType.MESH
F32 = jnp.float32
BF16 = jnp.bfloat16
LANES = 128
GROUP = 4


def make_tables(blocks, width):
    length = blocks * width
    half = blocks // 2
    block_of = np.concatenate([np.arange(half) * 2, np.arange(half) * 2 + 1]).astype(np.float64)
    k1 = np.arange(blocks, dtype=np.float64) + 0.25
    n2 = np.arange(width, dtype=np.float64)
    ang1 = 2.0 * np.pi * k1[:, None] * block_of[None, :] / blocks
    d1 = np.concatenate([np.cos(ang1), -np.sin(ang1)], axis=0)
    d4 = np.concatenate([np.cos(ang1), -np.sin(ang1)], axis=0).T
    ang2 = 2.0 * np.pi * k1[:, None] * n2[None, :] / length
    tw = np.concatenate([np.cos(ang2), np.sin(ang2)], axis=1)
    scale = 1.0 / (length * math.sqrt(length))
    ang3 = 2.0 * np.pi * n2[:, None] * n2[None, :] / width
    co, si = np.cos(ang3), np.sin(ang3)
    fwd = np.block([[co, -si], [si, co]])
    inv = np.block([[co, si], [-si, co]])
    return (
        jnp.asarray(d1, BF16),
        jnp.asarray(d4, BF16),
        jnp.asarray(np.concatenate([tw, tw * scale], axis=1), F32),
        jnp.asarray(fwd, BF16),
        jnp.asarray(inv, BF16),
    )


def kernel(
    blocks,
    v_hbm, gate_hbm, f_hbm, gy_hbm, d1_hbm, d4_hbm, tw_hbm, fwd_hbm, inv_hbm,
    gg_hbm, gv_hbm, gf_hbm,
    in_v, in_gate, in_f, in_gy, d1, d4, tw, fwd, inv,
    s_h, s_v, s_g, r_h, r_v, r_g,
    x32, y32, spec_h, spec_v, spec_g,
    s_c, s_gv, s_gf, r_pair, r_c, r_gv, r_gf,
    o_gg, o_gv, o_gf,
    in_sem, send_sem, recv_sem, out_sem,
):
    chans = in_v.shape[1]
    width = in_v.shape[0]
    ch = chans // blocks
    half = blocks // 2
    rows_half = half * ch
    d = lax.axis_index("dp")
    q = lax.axis_index("ctx")
    core = q % 2
    my_z, my_e = q // 4, q % 4
    zs = blocks // 4
    my_slot = core * half + q // 2

    loads = [
        pltpu.make_async_copy(src, dst, in_sem.at[i])
        for i, (src, dst) in enumerate(
            [
                (f_hbm, in_f), (v_hbm.at[0], in_v), (gy_hbm.at[0], in_gy), (gate_hbm.at[0], in_gate),
                (d1_hbm, d1), (tw_hbm, tw), (fwd_hbm, fwd), (inv_hbm, inv), (d4_hbm, d4),
            ]
        )
    ]
    for load in loads:
        load.start()

    def peer(k):
        step, e = k // 4, k % 4
        turn = step // 2
        dist = (turn + 1) // 2
        dz = jnp.where(turn % 2 == 1, zs - dist, dist) + (step % 2) * (zs // 2)
        return ((my_z + dz) % zs) * 4 + (my_e + e) % 4

    barrier = pltpu.get_barrier_semaphore()

    def greet(k, carry):
        pl.semaphore_signal(barrier, inc=1, device_id={"ctx": peer(k)}, device_id_type=MESH)
        return carry

    lax.fori_loop(1, blocks, greet, 0)
    pl.semaphore_signal(barrier, inc=1, device_id={"dp": 1 - d}, device_id_type=MESH)

    def rows(ref, start, count):
        return ref.at[pl.ds(pl.multiple_of(start, 16), count), :]

    def wait_bytes(ref, sem):
        pltpu.make_async_copy(ref, ref, sem).wait()

    def transpose_in(block_of, dst):
        for j in range(chans // LANES):
            dst[j * LANES:(j + 1) * LANES, :] = block_of(slice(j * LANES, (j + 1) * LANES)).T.astype(BF16)

    def send_in(src, dst, sem):
        pltpu.make_async_copy(rows(src, q * ch, ch), rows(dst, my_slot * ch, ch), recv_sem.at[sem]).start()

        def one(k, carry):
            to = peer(k)
            pltpu.make_async_remote_copy(
                src_ref=rows(src, to * ch, ch), dst_ref=rows(dst, my_slot * ch, ch),
                send_sem=send_sem.at[sem], recv_sem=recv_sem.at[sem],
                device_id={"ctx": to}, device_id_type=MESH,
            ).start()
            return carry

        lax.fori_loop(1, blocks, one, 0)

    def send_out(src, dst, sem, first=0, last=blocks):
        if first == 0:
            pltpu.make_async_copy(rows(src, my_slot * ch, ch), rows(dst, q * ch, ch), recv_sem.at[sem]).start()

        def one(k, carry):
            to = peer(k)
            slot = (to % 2) * half + to // 2
            pltpu.make_async_remote_copy(
                src_ref=rows(src, slot * ch, ch), dst_ref=rows(dst, q * ch, ch),
                send_sem=send_sem.at[sem], recv_sem=recv_sem.at[sem],
                device_id={"ctx": to}, device_id_type=MESH,
            ).start()
            return carry

        lax.fori_loop(max(first, 1), last, one, 0)

    def pair_copy(src, dst, sem):
        return pltpu.make_async_remote_copy(
            src_ref=src, dst_ref=dst, send_sem=send_sem.at[sem], recv_sem=recv_sem.at[sem],
            device_id={"dp": 1 - d}, device_id_type=MESH,
        )

    H, V, G, HP, CO, GV, GP, GF, GFP = range(9)

    loads[0].wait()
    transpose_in(lambda s: in_f[:, s].astype(F32), s_h)
    pl.semaphore_wait(barrier, blocks)

    @pl.when(core == d)
    def _():
        send_in(s_h, r_h, H)

    loads[1].wait()
    transpose_in(lambda s: in_v[:, s].astype(F32), s_v)
    send_in(s_v, r_v, V)
    loads[2].wait()
    loads[3].wait()
    transpose_in(lambda s: (in_gy[:, s].astype(F32) * in_gate[:, s].astype(F32)).astype(BF16).astype(F32), s_g)
    for load in loads[4:]:
        load.wait()

    def tw_at(i):
        return tw[:, i * LANES:(i + 1) * LANES]

    def forward(src, spec):
        x32[...] = src[...].astype(F32)
        for g in range(0, ch, GROUP):
            x = jnp.concatenate(
                [x32[pl.ds(c, blocks, stride=ch), :].astype(BF16) for c in range(g, g + GROUP)], axis=1
            )
            a = jnp.dot(d1[...], x, preferred_element_type=F32)
            turned = []
            for c in range(GROUP):
                re = a[:blocks, c * LANES:(c + 1) * LANES]
                im = a[blocks:, c * LANES:(c + 1) * LANES]
                turned.append(
                    jnp.concatenate(
                        [
                            (re * tw_at(0) + im * tw_at(1)).astype(BF16),
                            (im * tw_at(0) - re * tw_at(1)).astype(BF16),
                        ],
                        axis=1,
                    )
                )
            spec[g * blocks:(g + GROUP) * blocks, :] = jnp.dot(
                jnp.concatenate(turned, axis=0), fwd[...], preferred_element_type=F32
            )

    def inverse(left, right, sign, dst):
        for g in range(0, ch, GROUP):
            part = slice(g * blocks, (g + GROUP) * blocks)
            lr, li = left[part, :LANES], left[part, LANES:]
            rr, ri = right[part, :LANES], right[part, LANES:]
            if sign > 0:
                pr, pi = lr * rr - li * ri, lr * ri + li * rr
            else:
                pr, pi = lr * rr + li * ri, li * rr - lr * ri
            prod = jnp.concatenate([pr.astype(BF16), pi.astype(BF16)], axis=1)
            b = jnp.dot(prod, inv[...], preferred_element_type=F32)
            turned = []
            for c in range(GROUP):
                re = b[c * blocks:(c + 1) * blocks, :LANES]
                im = b[c * blocks:(c + 1) * blocks, LANES:]
                turned.append(
                    jnp.concatenate(
                        [
                            (re * tw_at(2) - im * tw_at(3)).astype(BF16),
                            (im * tw_at(2) + re * tw_at(3)).astype(BF16),
                        ],
                        axis=0,
                    )
                )
            y = jnp.dot(d4[...], jnp.concatenate(turned, axis=1), preferred_element_type=F32)
            for c in range(GROUP):
                y32[pl.ds(g + c, blocks, stride=ch), :] = y[:, c * LANES:(c + 1) * LANES]
        dst[...] = y32[...].astype(BF16)

    straight = rows(r_h, d * rows_half, rows_half)
    wait_bytes(straight, recv_sem.at[H])
    filter_pass = pair_copy(straight, straight, HP)
    filter_pass.start()
    send_in(s_g, r_g, G)
    wait_bytes(r_v, recv_sem.at[V])
    forward(r_v, spec_v)
    filter_pass.wait()
    forward(r_h, spec_h)
    inverse(spec_v, spec_h, 1, s_c)
    send_out(s_c, r_c, CO)

    wait_bytes(r_g, recv_sem.at[G])
    forward(r_g, spec_g)
    inverse(spec_g, spec_v, -1, s_gf)
    mine = rows(s_gf, d * rows_half, rows_half)
    grad_pass = pair_copy(rows(s_gf, (1 - d) * rows_half, rows_half), r_pair, GP)
    grad_pass.start()
    inverse(spec_g, spec_h, -1, s_gv)
    send_out(s_gv, r_gv, GV, 0, half)
    grad_pass.wait()
    at = pl.ds(pl.multiple_of(d * rows_half, 16), rows_half)
    s_gf[at, :] = (s_gf[at, :].astype(F32) + r_pair[...].astype(F32)).astype(BF16)

    def send_grad(k, carry):
        to = peer((k // 2) * 4 + (k % 2) * 2 + (core + d) % 2)
        slot = d * half + to // 2

        @pl.when(to != q)
        def _():
            pltpu.make_async_remote_copy(
                src_ref=rows(s_gf, slot * ch, ch), dst_ref=rows(r_gf, q * ch, ch),
                send_sem=send_sem.at[GF], recv_sem=recv_sem.at[GF],
                device_id={"ctx": to}, device_id_type=MESH,
            ).start()

        return carry

    lax.fori_loop(0, half, send_grad, 0)

    @pl.when(core == d)
    def _():
        pltpu.make_async_copy(rows(s_gf, my_slot * ch, ch), rows(r_gf, q * ch, ch), recv_sem.at[GF]).start()

    send_out(s_gv, r_gv, GV, half, blocks)

    wait_bytes(r_c, recv_sem.at[CO])
    for j in range(chans // LANES):
        s = slice(j * LANES, (j + 1) * LANES)
        o_gg[:, s] = (in_gy[:, s].astype(F32) * r_c[s, :].astype(F32).T).astype(BF16)
    out_gg = pltpu.make_async_copy(o_gg, gg_hbm.at[0], out_sem.at[0])
    out_gg.start()

    out_gf = pltpu.make_async_copy(o_gf, gf_hbm, out_sem.at[2])

    def give_gf():
        for j in range(chans // LANES):
            s = slice(j * LANES, (j + 1) * LANES)
            o_gf[:, s] = r_gf[s, :].astype(F32).T
        out_gf.start()

    @pl.when(core == d)
    def _():
        wait_bytes(r_gf, recv_sem.at[GF])
        pair_copy(r_gf, r_gf, GF).start()
        give_gf()

    wait_bytes(r_gv, recv_sem.at[GV])
    for j in range(chans // LANES):
        s = slice(j * LANES, (j + 1) * LANES)
        o_gv[:, s] = r_gv[s, :].astype(F32).T.astype(BF16)
    out_gv = pltpu.make_async_copy(o_gv, gv_hbm.at[0], out_sem.at[1])
    out_gv.start()

    @pl.when(core != d)
    def _():
        wait_bytes(r_gf, recv_sem.at[GF])
        give_gf()

    most = (blocks - 1) * ch

    @pl.when(core == d)
    def _():
        wait_bytes(s_h.at[pl.ds(0, most), :], send_sem.at[H])
        wait_bytes(s_gf.at[pl.ds(0, rows_half - ch), :], send_sem.at[GF])
        wait_bytes(r_gf, send_sem.at[GF])

    @pl.when(core != d)
    def _():
        wait_bytes(s_gf.at[pl.ds(0, rows_half), :], send_sem.at[GF])

    for ref, sem in ((s_v, V), (s_g, G), (s_c, CO), (s_gv, GV)):
        wait_bytes(ref.at[pl.ds(0, most), :], send_sem.at[sem])
    out_gg.wait()
    out_gv.wait()
    out_gf.wait()


def copy_kernel(*refs):
    count = len(refs) // 2
    sems = refs[-1]
    copies = [pltpu.make_async_copy(refs[i], refs[count + i], sems.at[i]) for i in range(count)]
    for copy in copies:
        copy.start()
    for copy in copies:
        copy.wait()


def body(values, gate_input, filter_param, grad_y, *tables):
    blocks = lax.axis_size("ctx")
    width, chans = filter_param.shape
    vm = lambda shape, kind: pltpu.VMEM(shape, kind)
    block = (width, chans)
    tiles = (chans, width)
    spec = (chans, 2 * width)
    any_spec = pl.BlockSpec(memory_space=pl.ANY)
    out_shape = (
        jax.ShapeDtypeStruct((1, width, chans), BF16),
        jax.ShapeDtypeStruct((1, width, chans), BF16),
        jax.ShapeDtypeStruct((width, chans), F32),
    )
    operands = [pltpu.with_memory_space_constraint(x, pltpu.HBM) for x in (values, gate_input, filter_param, grad_y, *tables)]
    results = pl.pallas_call(
        functools.partial(kernel, blocks),
        out_shape=out_shape,
        in_specs=[any_spec] * 9,
        out_specs=(any_spec,) * 3,
        scratch_shapes=[vm(block, BF16)] * 4
        + [vm(t.shape, t.dtype) for t in tables]
        + [vm(tiles, BF16)] * 6
        + [vm(tiles, F32)] * 2
        + [vm(spec, F32)] * 3
        + [vm(tiles, BF16)] * 3
        + [vm((chans // 2, width), BF16)]
        + [vm(tiles, BF16)] * 3
        + [vm(block, BF16)] * 2
        + [vm(block, F32)]
        + [
            pltpu.SemaphoreType.DMA((9,)),
            pltpu.SemaphoreType.DMA((9,)),
            pltpu.SemaphoreType.DMA((9,)),
            pltpu.SemaphoreType.DMA((3,)),
        ],
        compiler_params=pltpu.CompilerParams(
            collective_id=0, has_side_effects=True, vmem_limit_bytes=40 * 1024 * 1024
        ),
        cost_estimate=pl.CostEstimate(flops=1_000_000_000, bytes_accessed=4_000_000, transcendentals=0),
    )(*operands)
    return pl.pallas_call(
        copy_kernel,
        out_shape=out_shape,
        in_specs=[any_spec] * 3,
        out_specs=(any_spec,) * 3,
        scratch_shapes=[pltpu.SemaphoreType.DMA((3,))],
        compiler_params=pltpu.CompilerParams(vmem_limit_bytes=4 * 1024 * 1024),
    )(*results)


def solution(mesh):
    blocks = mesh.shape["ctx"]
    tables = make_tables(blocks, LANES)
    placed = (P("dp", "ctx", "tp"), P("dp", "ctx", "tp"), P("ctx", "tp"), P("dp", "ctx", "tp"))
    mapped = jax.shard_map(
        body,
        mesh=mesh,
        in_specs=placed + (P(),) * len(tables),
        out_specs=(P("dp", "ctx", "tp"), P("dp", "ctx", "tp"), P("ctx", "tp")),
        check_vma=False,
    )

    def run(values, gate_input, filter_param, grad_y):
        return mapped(values, gate_input, filter_param, grad_y, *tables)

    return run
```

```python
import functools
import math

import jax
import jax.numpy as jnp
import numpy as np
from jax import lax
from jax.experimental import pallas as pl
from jax.experimental.pallas import tpu as pltpu
from jax.sharding import PartitionSpec as P

MESH = pl.DeviceIdType.MESH
F32 = jnp.float32
BF16 = jnp.bfloat16
LANES = 128
GROUP = 4


def make_tables(blocks, width):
    length = blocks * width
    half = blocks // 2
    block_of = np.concatenate([np.arange(half) * 2, np.arange(half) * 2 + 1]).astype(np.float64)
    k1 = np.arange(blocks, dtype=np.float64) + 0.25
    n2 = np.arange(width, dtype=np.float64)
    ang1 = 2.0 * np.pi * k1[:, None] * block_of[None, :] / blocks
    d1 = np.concatenate([np.cos(ang1), -np.sin(ang1)], axis=0)
    d4 = np.concatenate([np.cos(ang1), -np.sin(ang1)], axis=0).T
    ang2 = 2.0 * np.pi * k1[:, None] * n2[None, :] / length
    tw = np.concatenate([np.cos(ang2), np.sin(ang2)], axis=1)
    scale = 1.0 / (length * math.sqrt(length))
    ang3 = 2.0 * np.pi * n2[:, None] * n2[None, :] / width
    co, si = np.cos(ang3), np.sin(ang3)
    fwd = np.block([[co, -si], [si, co]])
    inv = np.block([[co, si], [-si, co]])
    return (
        jnp.asarray(d1, BF16),
        jnp.asarray(d4, BF16),
        jnp.asarray(np.concatenate([tw, tw * scale], axis=1), F32),
        jnp.asarray(fwd, BF16),
        jnp.asarray(inv, BF16),
    )


def kernel(
    blocks,
    v_hbm, gate_hbm, f_hbm, gy_hbm, d1_hbm, d4_hbm, tw_hbm, fwd_hbm, inv_hbm,
    gg_hbm, gv_hbm, gf_hbm,
    in_v, in_gate, in_f, in_gy, d1, d4, tw, fwd, inv,
    s_h, s_v, s_g, r_h, r_v, r_g,
    x32, y32, spec_h, spec_v, spec_g,
    s_c, s_gv, s_gf, r_pair, r_c, r_gv, r_gf,
    o_gg, o_gv, o_gf,
    in_sem, send_sem, recv_sem, out_sem,
):
    chans = in_v.shape[1]
    width = in_v.shape[0]
    ch = chans // blocks
    half = blocks // 2
    rows_half = half * ch
    d = lax.axis_index("dp")
    q = lax.axis_index("ctx")
    core = q % 2
    my_z, my_e = q // 4, q % 4
    zs = blocks // 4
    my_slot = core * half + q // 2

    loads = [
        pltpu.make_async_copy(src, dst, in_sem.at[i])
        for i, (src, dst) in enumerate(
            [
                (f_hbm, in_f), (v_hbm.at[0], in_v), (gy_hbm.at[0], in_gy), (gate_hbm.at[0], in_gate),
                (d1_hbm, d1), (tw_hbm, tw), (fwd_hbm, fwd), (inv_hbm, inv), (d4_hbm, d4),
            ]
        )
    ]
    loads[0].start()

    def peer(k, turned=0):
        step, e = k // 4, k % 4
        turn = step // 2
        dist = (turn + 1) // 2
        dz = (zs - dist if turn % 2 else dist) + step % 2 * (zs // 2)
        return lax.rem(my_z + dz, zs) * 4 + lax.rem(my_e + e + turned, 4)

    barrier = pltpu.get_barrier_semaphore()

    for k in range(1, blocks):
        pl.semaphore_signal(barrier, inc=1, device_id={"ctx": peer(k)}, device_id_type=MESH)
    pl.semaphore_signal(barrier, inc=1, device_id={"dp": 1 - d}, device_id_type=MESH)
    for load in loads[1:]:
        load.start()

    def rows(ref, start, count):
        return ref.at[pl.ds(pl.multiple_of(start, 16), count), :]

    def wait_bytes(ref, sem):
        pltpu.make_async_copy(ref, ref, sem).wait()

    def transpose_in(block_of, dst):
        for j in range(chans // LANES):
            dst[j * LANES:(j + 1) * LANES, :] = block_of(slice(j * LANES, (j + 1) * LANES)).T.astype(BF16)

    def send_in(src, dst, sem):
        pltpu.make_async_copy(rows(src, q * ch, ch), rows(dst, my_slot * ch, ch), recv_sem.at[sem]).start()

        for k in range(1, blocks):
            to = peer(k)
            pltpu.make_async_remote_copy(
                src_ref=rows(src, to * ch, ch), dst_ref=rows(dst, my_slot * ch, ch),
                send_sem=send_sem.at[sem], recv_sem=recv_sem.at[sem],
                device_id={"ctx": to}, device_id_type=MESH,
            ).start()

    def send_out(src, dst, sem, first=0, last=blocks):
        if first == 0:
            pltpu.make_async_copy(rows(src, my_slot * ch, ch), rows(dst, q * ch, ch), recv_sem.at[sem]).start()

        for k in range(max(first, 1), last):
            to = peer(k)
            slot = lax.rem(to, 2) * half + lax.div(to, 2)
            pltpu.make_async_remote_copy(
                src_ref=rows(src, slot * ch, ch), dst_ref=rows(dst, q * ch, ch),
                send_sem=send_sem.at[sem], recv_sem=recv_sem.at[sem],
                device_id={"ctx": to}, device_id_type=MESH,
            ).start()

    def pair_copy(src, dst, sem):
        return pltpu.make_async_remote_copy(
            src_ref=src, dst_ref=dst, send_sem=send_sem.at[sem], recv_sem=recv_sem.at[sem],
            device_id={"dp": 1 - d}, device_id_type=MESH,
        )

    H, V, G, HP, CO, GV, GP, GF, GFP = range(9)

    loads[0].wait()

    @pl.when(core == d)
    def _():
        transpose_in(lambda s: in_f[:, s].astype(F32), s_h)

    pl.semaphore_wait(barrier, blocks)

    @pl.when(core == d)
    def _():
        send_in(s_h, r_h, H)

    loads[1].wait()
    transpose_in(lambda s: in_v[:, s].astype(F32), s_v)
    send_in(s_v, r_v, V)
    loads[2].wait()
    loads[3].wait()
    transpose_in(lambda s: (in_gy[:, s].astype(F32) * in_gate[:, s].astype(F32)).astype(BF16).astype(F32), s_g)
    for load in loads[4:]:
        load.wait()

    def tw_at(i):
        return tw[:, i * LANES:(i + 1) * LANES]

    def forward(src, spec):
        x32[...] = src[...].astype(F32)
        for g in range(0, ch, GROUP):
            x = jnp.concatenate(
                [x32[pl.ds(c, blocks, stride=ch), :].astype(BF16) for c in range(g, g + GROUP)], axis=1
            )
            a = jnp.dot(d1[...], x, preferred_element_type=F32)
            turned = []
            for c in range(GROUP):
                re = a[:blocks, c * LANES:(c + 1) * LANES]
                im = a[blocks:, c * LANES:(c + 1) * LANES]
                turned.append(
                    jnp.concatenate(
                        [
                            (re * tw_at(0) + im * tw_at(1)).astype(BF16),
                            (im * tw_at(0) - re * tw_at(1)).astype(BF16),
                        ],
                        axis=1,
                    )
                )
            spec[g * blocks:(g + GROUP) * blocks, :] = jnp.dot(
                jnp.concatenate(turned, axis=0), fwd[...], preferred_element_type=F32
            )

    def inverse(left, right, sign, dst):
        for g in range(0, ch, GROUP):
            part = slice(g * blocks, (g + GROUP) * blocks)
            lr, li = left[part, :LANES], left[part, LANES:]
            rr, ri = right[part, :LANES], right[part, LANES:]
            if sign > 0:
                pr, pi = lr * rr - li * ri, lr * ri + li * rr
            else:
                pr, pi = lr * rr + li * ri, li * rr - lr * ri
            prod = jnp.concatenate([pr.astype(BF16), pi.astype(BF16)], axis=1)
            b = jnp.dot(prod, inv[...], preferred_element_type=F32)
            turned = []
            for c in range(GROUP):
                re = b[c * blocks:(c + 1) * blocks, :LANES]
                im = b[c * blocks:(c + 1) * blocks, LANES:]
                turned.append(
                    jnp.concatenate(
                        [
                            (re * tw_at(2) - im * tw_at(3)).astype(BF16),
                            (im * tw_at(2) + re * tw_at(3)).astype(BF16),
                        ],
                        axis=0,
                    )
                )
            y = jnp.dot(d4[...], jnp.concatenate(turned, axis=1), preferred_element_type=F32)
            for c in range(GROUP):
                y32[pl.ds(g + c, blocks, stride=ch), :] = y[:, c * LANES:(c + 1) * LANES]
        dst[...] = y32[...].astype(BF16)

    straight = rows(r_h, d * rows_half, rows_half)
    wait_bytes(straight, recv_sem.at[H])
    filter_pass = pair_copy(straight, straight, HP)
    filter_pass.start()
    send_in(s_g, r_g, G)
    wait_bytes(r_v, recv_sem.at[V])
    forward(r_v, spec_v)
    filter_pass.wait()
    forward(r_h, spec_h)
    inverse(spec_v, spec_h, 1, s_c)
    send_out(s_c, r_c, CO)

    wait_bytes(r_g, recv_sem.at[G])
    forward(r_g, spec_g)
    inverse(spec_g, spec_v, -1, s_gf)
    mine = rows(s_gf, d * rows_half, rows_half)
    grad_pass = pair_copy(rows(s_gf, (1 - d) * rows_half, rows_half), r_pair, GP)
    grad_pass.start()
    inverse(spec_g, spec_h, -1, s_gv)
    send_out(s_gv, r_gv, GV, 0, half)
    grad_pass.wait()
    at = pl.ds(pl.multiple_of(d * rows_half, 16), rows_half)
    s_gf[at, :] = (s_gf[at, :].astype(F32) + r_pair[...].astype(F32)).astype(BF16)

    odd = lax.rem(core + d, 2)

    def send_grad(k):
        to = peer(k, odd)
        pltpu.make_async_remote_copy(
            src_ref=rows(s_gf, (d * half + lax.div(to, 2)) * ch, ch), dst_ref=rows(r_gf, q * ch, ch),
            send_sem=send_sem.at[GF], recv_sem=recv_sem.at[GF],
            device_id={"ctx": to}, device_id_type=MESH,
        ).start()

    for k in range(2, blocks, 2):
        send_grad(k)

    @pl.when(core == d)
    def _():
        pltpu.make_async_copy(rows(s_gf, my_slot * ch, ch), rows(r_gf, q * ch, ch), recv_sem.at[GF]).start()

    @pl.when(core != d)
    def _():
        send_grad(0)

    send_out(s_gv, r_gv, GV, half, blocks)

    wait_bytes(r_c, recv_sem.at[CO])
    for j in range(chans // LANES):
        s = slice(j * LANES, (j + 1) * LANES)
        o_gg[:, s] = (in_gy[:, s].astype(F32) * r_c[s, :].astype(F32).T).astype(BF16)
    out_gg = pltpu.make_async_copy(o_gg, gg_hbm.at[0], out_sem.at[0])
    out_gg.start()

    out_gf = pltpu.make_async_copy(o_gf, gf_hbm, out_sem.at[2])

    def give_gf():
        for j in range(chans // LANES):
            s = slice(j * LANES, (j + 1) * LANES)
            o_gf[:, s] = r_gf[s, :].astype(F32).T
        out_gf.start()

    @pl.when(core == d)
    def _():
        wait_bytes(r_gf, recv_sem.at[GF])
        pair_copy(r_gf, r_gf, GF).start()
        give_gf()

    wait_bytes(r_gv, recv_sem.at[GV])
    for j in range(chans // LANES):
        s = slice(j * LANES, (j + 1) * LANES)
        o_gv[:, s] = r_gv[s, :].astype(F32).T.astype(BF16)
    out_gv = pltpu.make_async_copy(o_gv, gv_hbm.at[0], out_sem.at[1])
    out_gv.start()

    @pl.when(core != d)
    def _():
        wait_bytes(r_gf, recv_sem.at[GF])
        give_gf()

    most = (blocks - 1) * ch

    @pl.when(core == d)
    def _():
        wait_bytes(s_h.at[pl.ds(0, most), :], send_sem.at[H])
        wait_bytes(s_gf.at[pl.ds(0, rows_half - ch), :], send_sem.at[GF])
        wait_bytes(r_gf, send_sem.at[GF])

    @pl.when(core != d)
    def _():
        wait_bytes(s_gf.at[pl.ds(0, rows_half), :], send_sem.at[GF])

    for ref, sem in ((s_v, V), (s_g, G), (s_c, CO), (s_gv, GV)):
        wait_bytes(ref.at[pl.ds(0, most), :], send_sem.at[sem])
    out_gg.wait()
    out_gv.wait()
    out_gf.wait()


def copy_kernel(*refs):
    count = len(refs) // 2
    sems = refs[-1]
    copies = [pltpu.make_async_copy(refs[i], refs[count + i], sems.at[i]) for i in range(count)]
    for copy in copies:
        copy.start()
    for copy in copies:
        copy.wait()


def body(values, gate_input, filter_param, grad_y, *tables):
    blocks = lax.axis_size("ctx")
    width, chans = filter_param.shape
    vm = lambda shape, kind: pltpu.VMEM(shape, kind)
    block = (width, chans)
    tiles = (chans, width)
    spec = (chans, 2 * width)
    any_spec = pl.BlockSpec(memory_space=pl.ANY)
    out_shape = (
        jax.ShapeDtypeStruct((1, width, chans), BF16),
        jax.ShapeDtypeStruct((1, width, chans), BF16),
        jax.ShapeDtypeStruct((width, chans), F32),
    )
    operands = [pltpu.with_memory_space_constraint(x, pltpu.HBM) for x in (values, gate_input, filter_param, grad_y, *tables)]
    results = pl.pallas_call(
        functools.partial(kernel, blocks),
        out_shape=out_shape,
        in_specs=[any_spec] * 9,
        out_specs=(any_spec,) * 3,
        scratch_shapes=[vm(block, BF16)] * 4
        + [vm(t.shape, t.dtype) for t in tables]
        + [vm(tiles, BF16)] * 6
        + [vm(tiles, F32)] * 2
        + [vm(spec, F32)] * 3
        + [vm(tiles, BF16)] * 3
        + [vm((chans // 2, width), BF16)]
        + [vm(tiles, BF16)] * 3
        + [vm(block, BF16)] * 2
        + [vm(block, F32)]
        + [
            pltpu.SemaphoreType.DMA((9,)),
            pltpu.SemaphoreType.DMA((9,)),
            pltpu.SemaphoreType.DMA((9,)),
            pltpu.SemaphoreType.DMA((3,)),
        ],
        compiler_params=pltpu.CompilerParams(
            collective_id=0, has_side_effects=True, vmem_limit_bytes=40 * 1024 * 1024
        ),
        cost_estimate=pl.CostEstimate(flops=1_000_000_000, bytes_accessed=4_000_000, transcendentals=0),
    )(*operands)
    return pl.pallas_call(
        copy_kernel,
        out_shape=out_shape,
        in_specs=[any_spec] * 3,
        out_specs=(any_spec,) * 3,
        scratch_shapes=[pltpu.SemaphoreType.DMA((3,))],
        compiler_params=pltpu.CompilerParams(vmem_limit_bytes=4 * 1024 * 1024),
    )(*results)


def solution(mesh):
    blocks = mesh.shape["ctx"]
    tables = make_tables(blocks, LANES)
    placed = (P("dp", "ctx", "tp"), P("dp", "ctx", "tp"), P("ctx", "tp"), P("dp", "ctx", "tp"))
    mapped = jax.shard_map(
        body,
        mesh=mesh,
        in_specs=placed + (P(),) * len(tables),
        out_specs=(P("dp", "ctx", "tp"), P("dp", "ctx", "tp"), P("ctx", "tp")),
        check_vma=False,
    )

    def run(values, gate_input, filter_param, grad_y):
        return mapped(values, gate_input, filter_param, grad_y, *tables)

    return run
```

```python
import functools
import math

import jax
import jax.numpy as jnp
import ml_dtypes
import numpy as np
from jax import lax
from jax.experimental import pallas as pl
from jax.experimental.pallas import tpu as pltpu
from jax.sharding import PartitionSpec as P

MESH = pl.DeviceIdType.MESH
F32 = jnp.float32
BF16 = jnp.bfloat16
LANES = 128
GROUP = 4


def make_tables(blocks, width):
    length = blocks * width
    half = blocks // 2
    block_of = np.concatenate([np.arange(half) * 2, np.arange(half) * 2 + 1]).astype(np.float64)
    k1 = np.arange(blocks, dtype=np.float64) + 0.25
    n2 = np.arange(width, dtype=np.float64)
    ang1 = 2.0 * np.pi * k1[:, None] * block_of[None, :] / blocks
    d1 = np.concatenate([np.cos(ang1), -np.sin(ang1)], axis=0)
    d4 = np.concatenate([np.cos(ang1), -np.sin(ang1)], axis=0).T
    ang2 = 2.0 * np.pi * k1[:, None] * n2[None, :] / length
    tw = np.concatenate([np.cos(ang2), np.sin(ang2)], axis=1)
    scale = 1.0 / (length * math.sqrt(length))
    ang3 = 2.0 * np.pi * n2[:, None] * n2[None, :] / width
    co, si = np.cos(ang3), np.sin(ang3)
    fwd = np.block([[co, -si], [si, co]])
    inv = np.block([[co, si], [-si, co]])

    def two_parts(table, axis):
        high = np.asarray(table, ml_dtypes.bfloat16)
        low = np.asarray(table - high.astype(np.float64), ml_dtypes.bfloat16)
        return jnp.asarray(np.concatenate([high, low], axis=axis))

    return (
        two_parts(d1, 1),
        two_parts(d4, 1),
        jnp.asarray(np.concatenate([tw, tw * scale], axis=1), F32),
        jnp.asarray(fwd, BF16),
        jnp.asarray(inv, BF16),
    )


def kernel(
    blocks,
    v_hbm, gate_hbm, f_hbm, gy_hbm, d1_hbm, d4_hbm, tw_hbm, fwd_hbm, inv_hbm,
    gg_hbm, gv_hbm, gf_hbm,
    in_v, in_gate, in_f, in_gy, d1, d4, tw, fwd, inv,
    s_h, s_v, s_g, r_h, r_v, r_g,
    x32, y32, spec_h, spec_v, spec_g,
    s_c, s_gv, s_gf, r_pair, r_c, r_gv, r_gf,
    o_gg, o_gv, o_gf,
    in_sem, send_sem, recv_sem, out_sem,
):
    chans = in_v.shape[1]
    width = in_v.shape[0]
    ch = chans // blocks
    half = blocks // 2
    rows_half = half * ch
    d = lax.axis_index("dp")
    q = lax.axis_index("ctx")
    core = q % 2
    my_z, my_e = q // 4, q % 4
    zs = blocks // 4
    my_slot = core * half + q // 2

    loads = [
        pltpu.make_async_copy(src, dst, in_sem.at[i])
        for i, (src, dst) in enumerate(
            [
                (f_hbm, in_f), (v_hbm.at[0], in_v), (gy_hbm.at[0], in_gy), (gate_hbm.at[0], in_gate),
                (d1_hbm, d1), (tw_hbm, tw), (fwd_hbm, fwd), (inv_hbm, inv), (d4_hbm, d4),
            ]
        )
    ]
    loads[0].start()

    def peer(k, turned=0):
        step, e = k // 4, k % 4
        turn = step // 2
        dist = (turn + 1) // 2
        dz = (zs - dist if turn % 2 else dist) + step % 2 * (zs // 2)
        return lax.rem(my_z + dz, zs) * 4 + lax.rem(my_e + e + turned, 4)

    barrier = pltpu.get_barrier_semaphore()

    for k in range(1, blocks):
        pl.semaphore_signal(barrier, inc=1, device_id={"ctx": peer(k)}, device_id_type=MESH)
    pl.semaphore_signal(barrier, inc=1, device_id={"dp": 1 - d}, device_id_type=MESH)
    for load in loads[1:]:
        load.start()

    def rows(ref, start, count):
        return ref.at[pl.ds(pl.multiple_of(start, 16), count), :]

    def wait_bytes(ref, sem):
        pltpu.make_async_copy(ref, ref, sem).wait()

    def transpose_in(block_of, dst):
        for j in range(chans // LANES):
            dst[j * LANES:(j + 1) * LANES, :] = block_of(slice(j * LANES, (j + 1) * LANES)).T.astype(BF16)

    def send_in(src, dst, sem):
        pltpu.make_async_copy(rows(src, q * ch, ch), rows(dst, my_slot * ch, ch), recv_sem.at[sem]).start()

        for k in range(1, blocks):
            to = peer(k)
            pltpu.make_async_remote_copy(
                src_ref=rows(src, to * ch, ch), dst_ref=rows(dst, my_slot * ch, ch),
                send_sem=send_sem.at[sem], recv_sem=recv_sem.at[sem],
                device_id={"ctx": to}, device_id_type=MESH,
            ).start()

    def send_out(src, dst, sem, first=0, last=blocks):
        if first == 0:
            pltpu.make_async_copy(rows(src, my_slot * ch, ch), rows(dst, q * ch, ch), recv_sem.at[sem]).start()

        for k in range(max(first, 1), last):
            to = peer(k)
            slot = lax.rem(to, 2) * half + lax.div(to, 2)
            pltpu.make_async_remote_copy(
                src_ref=rows(src, slot * ch, ch), dst_ref=rows(dst, q * ch, ch),
                send_sem=send_sem.at[sem], recv_sem=recv_sem.at[sem],
                device_id={"ctx": to}, device_id_type=MESH,
            ).start()

    def pair_copy(src, dst, sem):
        return pltpu.make_async_remote_copy(
            src_ref=src, dst_ref=dst, send_sem=send_sem.at[sem], recv_sem=recv_sem.at[sem],
            device_id={"dp": 1 - d}, device_id_type=MESH,
        )

    H, V, G, HP, CO, GV, GP, GF, GFP = range(9)

    loads[0].wait()

    @pl.when(core == d)
    def _():
        transpose_in(lambda s: in_f[:, s].astype(F32), s_h)

    pl.semaphore_wait(barrier, blocks)

    @pl.when(core == d)
    def _():
        send_in(s_h, r_h, H)

    loads[1].wait()
    transpose_in(lambda s: in_v[:, s].astype(F32), s_v)
    send_in(s_v, r_v, V)
    loads[2].wait()
    loads[3].wait()
    transpose_in(lambda s: (in_gy[:, s].astype(F32) * in_gate[:, s].astype(F32)).astype(BF16).astype(F32), s_g)
    for load in loads[4:]:
        load.wait()

    def tw_at(i):
        return tw[:, i * LANES:(i + 1) * LANES]

    def two_dots(left, table):
        return jnp.dot(left, table[...], preferred_element_type=F32)

    def forward(src, spec):
        x32[...] = src[...].astype(F32)
        for g in range(0, ch, GROUP):
            x = jnp.concatenate(
                [x32[pl.ds(c, blocks, stride=ch), :].astype(BF16) for c in range(g, g + GROUP)], axis=1
            )
            a = jnp.dot(d1[...], jnp.concatenate([x, x], axis=0), preferred_element_type=F32)
            turned = []
            for c in range(GROUP):
                re = a[:blocks, c * LANES:(c + 1) * LANES]
                im = a[blocks:, c * LANES:(c + 1) * LANES]
                turned.append(
                    jnp.concatenate(
                        [
                            (re * tw_at(0) + im * tw_at(1)).astype(BF16),
                            (im * tw_at(0) - re * tw_at(1)).astype(BF16),
                        ],
                        axis=1,
                    )
                )
            spec[g * blocks:(g + GROUP) * blocks, :] = two_dots(jnp.concatenate(turned, axis=0), fwd)

    def inverse(left, right, sign, dst):
        for g in range(0, ch, GROUP):
            part = slice(g * blocks, (g + GROUP) * blocks)
            lr, li = left[part, :LANES], left[part, LANES:]
            rr, ri = right[part, :LANES], right[part, LANES:]
            if sign > 0:
                pr, pi = lr * rr - li * ri, lr * ri + li * rr
            else:
                pr, pi = lr * rr + li * ri, li * rr - lr * ri
            prod = jnp.concatenate([pr.astype(BF16), pi.astype(BF16)], axis=1)
            b = two_dots(prod, inv)
            turned = []
            for c in range(GROUP):
                re = b[c * blocks:(c + 1) * blocks, :LANES]
                im = b[c * blocks:(c + 1) * blocks, LANES:]
                turned.append(
                    jnp.concatenate(
                        [
                            (re * tw_at(2) - im * tw_at(3)).astype(BF16),
                            (im * tw_at(2) + re * tw_at(3)).astype(BF16),
                        ],
                        axis=0,
                    )
                )
            both = jnp.concatenate(turned, axis=1)
            y = jnp.dot(d4[...], jnp.concatenate([both, both], axis=0), preferred_element_type=F32)
            for c in range(GROUP):
                y32[pl.ds(g + c, blocks, stride=ch), :] = y[:, c * LANES:(c + 1) * LANES]
        dst[...] = y32[...].astype(BF16)

    straight = rows(r_h, d * rows_half, rows_half)
    wait_bytes(straight, recv_sem.at[H])
    filter_pass = pair_copy(straight, straight, HP)
    filter_pass.start()
    send_in(s_g, r_g, G)
    wait_bytes(r_v, recv_sem.at[V])
    forward(r_v, spec_v)
    filter_pass.wait()
    forward(r_h, spec_h)
    inverse(spec_v, spec_h, 1, s_c)
    send_out(s_c, r_c, CO)

    wait_bytes(r_g, recv_sem.at[G])
    forward(r_g, spec_g)
    inverse(spec_g, spec_v, -1, s_gf)
    mine = rows(s_gf, d * rows_half, rows_half)
    grad_pass = pair_copy(rows(s_gf, (1 - d) * rows_half, rows_half), r_pair, GP)
    grad_pass.start()
    inverse(spec_g, spec_h, -1, s_gv)
    send_out(s_gv, r_gv, GV, 0, half)
    grad_pass.wait()
    at = pl.ds(pl.multiple_of(d * rows_half, 16), rows_half)
    s_gf[at, :] = (s_gf[at, :].astype(F32) + r_pair[...].astype(F32)).astype(BF16)

    odd = lax.rem(core + d, 2)

    def send_grad(k):
        to = peer(k, odd)
        pltpu.make_async_remote_copy(
            src_ref=rows(s_gf, (d * half + lax.div(to, 2)) * ch, ch), dst_ref=rows(r_gf, q * ch, ch),
            send_sem=send_sem.at[GF], recv_sem=recv_sem.at[GF],
            device_id={"ctx": to}, device_id_type=MESH,
        ).start()

    for k in range(2, blocks, 2):
        send_grad(k)

    @pl.when(core == d)
    def _():
        pltpu.make_async_copy(rows(s_gf, my_slot * ch, ch), rows(r_gf, q * ch, ch), recv_sem.at[GF]).start()

    @pl.when(core != d)
    def _():
        send_grad(0)

    send_out(s_gv, r_gv, GV, half, blocks)

    wait_bytes(r_c, recv_sem.at[CO])
    for j in range(chans // LANES):
        s = slice(j * LANES, (j + 1) * LANES)
        o_gg[:, s] = (in_gy[:, s].astype(F32) * r_c[s, :].astype(F32).T).astype(BF16)
    out_gg = pltpu.make_async_copy(o_gg, gg_hbm.at[0], out_sem.at[0])
    out_gg.start()

    out_gf = pltpu.make_async_copy(o_gf, gf_hbm, out_sem.at[2])

    def give_gf():
        for j in range(chans // LANES):
            s = slice(j * LANES, (j + 1) * LANES)
            o_gf[:, s] = r_gf[s, :].astype(F32).T
        out_gf.start()

    @pl.when(core == d)
    def _():
        wait_bytes(r_gf, recv_sem.at[GF])
        pair_copy(r_gf, r_gf, GF).start()
        give_gf()

    wait_bytes(r_gv, recv_sem.at[GV])
    for j in range(chans // LANES):
        s = slice(j * LANES, (j + 1) * LANES)
        o_gv[:, s] = r_gv[s, :].astype(F32).T.astype(BF16)
    out_gv = pltpu.make_async_copy(o_gv, gv_hbm.at[0], out_sem.at[1])
    out_gv.start()

    @pl.when(core != d)
    def _():
        wait_bytes(r_gf, recv_sem.at[GF])
        give_gf()

    most = (blocks - 1) * ch

    @pl.when(core == d)
    def _():
        wait_bytes(s_h.at[pl.ds(0, most), :], send_sem.at[H])
        wait_bytes(s_gf.at[pl.ds(0, rows_half - ch), :], send_sem.at[GF])
        wait_bytes(r_gf, send_sem.at[GF])

    @pl.when(core != d)
    def _():
        wait_bytes(s_gf.at[pl.ds(0, rows_half), :], send_sem.at[GF])

    for ref, sem in ((s_v, V), (s_g, G), (s_c, CO), (s_gv, GV)):
        wait_bytes(ref.at[pl.ds(0, most), :], send_sem.at[sem])
    out_gg.wait()
    out_gv.wait()
    out_gf.wait()


def copy_kernel(*refs):
    count = len(refs) // 2
    sems = refs[-1]
    copies = [pltpu.make_async_copy(refs[i], refs[count + i], sems.at[i]) for i in range(count)]
    for copy in copies:
        copy.start()
    for copy in copies:
        copy.wait()


def body(values, gate_input, filter_param, grad_y, *tables):
    blocks = lax.axis_size("ctx")
    width, chans = filter_param.shape
    vm = lambda shape, kind: pltpu.VMEM(shape, kind)
    block = (width, chans)
    tiles = (chans, width)
    spec = (chans, 2 * width)
    any_spec = pl.BlockSpec(memory_space=pl.ANY)
    out_shape = (
        jax.ShapeDtypeStruct((1, width, chans), BF16),
        jax.ShapeDtypeStruct((1, width, chans), BF16),
        jax.ShapeDtypeStruct((width, chans), F32),
    )
    operands = [pltpu.with_memory_space_constraint(x, pltpu.HBM) for x in (values, gate_input, filter_param, grad_y, *tables)]
    results = pl.pallas_call(
        functools.partial(kernel, blocks),
        out_shape=out_shape,
        in_specs=[any_spec] * 9,
        out_specs=(any_spec,) * 3,
        scratch_shapes=[vm(block, BF16)] * 4
        + [vm(t.shape, t.dtype) for t in tables]
        + [vm(tiles, BF16)] * 6
        + [vm(tiles, F32)] * 2
        + [vm(spec, F32)] * 3
        + [vm(tiles, BF16)] * 3
        + [vm((chans // 2, width), BF16)]
        + [vm(tiles, BF16)] * 3
        + [vm(block, BF16)] * 2
        + [vm(block, F32)]
        + [
            pltpu.SemaphoreType.DMA((9,)),
            pltpu.SemaphoreType.DMA((9,)),
            pltpu.SemaphoreType.DMA((9,)),
            pltpu.SemaphoreType.DMA((3,)),
        ],
        compiler_params=pltpu.CompilerParams(
            collective_id=0, has_side_effects=True, vmem_limit_bytes=40 * 1024 * 1024
        ),
        cost_estimate=pl.CostEstimate(flops=1_000_000_000, bytes_accessed=4_000_000, transcendentals=0),
    )(*operands)
    return pl.pallas_call(
        copy_kernel,
        out_shape=out_shape,
        in_specs=[any_spec] * 3,
        out_specs=(any_spec,) * 3,
        scratch_shapes=[pltpu.SemaphoreType.DMA((3,))],
        compiler_params=pltpu.CompilerParams(vmem_limit_bytes=4 * 1024 * 1024),
    )(*results)


def solution(mesh):
    blocks = mesh.shape["ctx"]
    tables = make_tables(blocks, LANES)
    placed = (P("dp", "ctx", "tp"), P("dp", "ctx", "tp"), P("ctx", "tp"), P("dp", "ctx", "tp"))
    mapped = jax.shard_map(
        body,
        mesh=mesh,
        in_specs=placed + (P(),) * len(tables),
        out_specs=(P("dp", "ctx", "tp"), P("dp", "ctx", "tp"), P("ctx", "tp")),
        check_vma=False,
    )

    def run(values, gate_input, filter_param, grad_y):
        return mapped(values, gate_input, filter_param, grad_y, *tables)

    return run
```

```python
import functools
import math

import jax
import jax.numpy as jnp
import ml_dtypes
import numpy as np
from jax import lax
from jax.experimental import pallas as pl
from jax.experimental.pallas import tpu as pltpu
from jax.sharding import PartitionSpec as P

MESH = pl.DeviceIdType.MESH
F32 = jnp.float32
BF16 = jnp.bfloat16
LANES = 128
GROUP = 4


def make_tables(blocks, width):
    length = blocks * width
    half = blocks // 2
    block_of = np.concatenate([np.arange(half) * 2, np.arange(half) * 2 + 1]).astype(np.float64)
    k1 = np.arange(blocks, dtype=np.float64) + 0.25
    n2 = np.arange(width, dtype=np.float64)
    ang1 = 2.0 * np.pi * k1[:, None] * block_of[None, :] / blocks
    d1 = np.concatenate([np.cos(ang1), -np.sin(ang1)], axis=0)
    d4 = np.concatenate([np.cos(ang1), -np.sin(ang1)], axis=0).T
    ang2 = 2.0 * np.pi * k1[:, None] * n2[None, :] / length
    tw = np.concatenate([np.cos(ang2), np.sin(ang2)], axis=1)
    scale = 1.0 / (length * math.sqrt(length))
    ang3 = 2.0 * np.pi * n2[:, None] * n2[None, :] / width
    co, si = np.cos(ang3), np.sin(ang3)
    fwd = np.block([[co, -si], [si, co]])
    inv = np.block([[co, si], [-si, co]])

    def two_parts(table, axis):
        high = np.asarray(table, ml_dtypes.bfloat16)
        low = np.asarray(table - high.astype(np.float64), ml_dtypes.bfloat16)
        return jnp.asarray(np.concatenate([high, low], axis=axis))

    return (
        two_parts(d1, 1),
        two_parts(d4, 1),
        jnp.asarray(np.concatenate([tw, tw * scale], axis=1), F32),
        jnp.asarray(fwd, BF16),
        jnp.asarray(inv, BF16),
    )


def kernel(
    blocks,
    v_hbm, gate_hbm, f_hbm, gy_hbm, d1_hbm, d4_hbm, tw_hbm, fwd_hbm, inv_hbm,
    o_gg, o_gv, o_gf,
    in_v, in_gate, in_f, in_gy, d1, d4, tw, fwd, inv,
    s_h, s_v, s_g, r_h, r_v, r_g,
    x32, y32, spec_h, spec_v, spec_g,
    s_c, s_gv, s_gf, r_pair, r_c, r_gv, r_gf,
    in_sem, send_sem, recv_sem,
):
    chans = in_v.shape[1]
    width = in_v.shape[0]
    ch = chans // blocks
    half = blocks // 2
    rows_half = half * ch
    d = lax.axis_index("dp")
    q = lax.axis_index("ctx")
    core = q % 2
    my_z, my_e = q // 4, q % 4
    zs = blocks // 4
    my_slot = core * half + q // 2

    loads = [
        pltpu.make_async_copy(src, dst, in_sem.at[i])
        for i, (src, dst) in enumerate(
            [
                (f_hbm, in_f), (v_hbm.at[0], in_v), (gy_hbm.at[0], in_gy), (gate_hbm.at[0], in_gate),
                (d1_hbm, d1), (tw_hbm, tw), (fwd_hbm, fwd), (inv_hbm, inv), (d4_hbm, d4),
            ]
        )
    ]
    loads[0].start()

    def peer(k, turned=0):
        step, e = k // 4, k % 4
        turn = step // 2
        dist = (turn + 1) // 2
        dz = (zs - dist if turn % 2 else dist) + step % 2 * (zs // 2)
        return lax.rem(my_z + dz, zs) * 4 + lax.rem(my_e + e + turned, 4)

    barrier = pltpu.get_barrier_semaphore()

    for k in range(1, blocks):
        pl.semaphore_signal(barrier, inc=1, device_id={"ctx": peer(k)}, device_id_type=MESH)
    pl.semaphore_signal(barrier, inc=1, device_id={"dp": 1 - d}, device_id_type=MESH)
    for load in loads[1:]:
        load.start()

    def rows(ref, start, count):
        return ref.at[pl.ds(pl.multiple_of(start, 16), count), :]

    def wait_bytes(ref, sem):
        pltpu.make_async_copy(ref, ref, sem).wait()

    def transpose_in(block_of, dst):
        for j in range(chans // LANES):
            dst[j * LANES:(j + 1) * LANES, :] = block_of(slice(j * LANES, (j + 1) * LANES)).T.astype(BF16)

    def send_in(src, dst, sem):
        pltpu.make_async_copy(rows(src, q * ch, ch), rows(dst, my_slot * ch, ch), recv_sem.at[sem]).start()

        for k in range(1, blocks):
            to = peer(k)
            pltpu.make_async_remote_copy(
                src_ref=rows(src, to * ch, ch), dst_ref=rows(dst, my_slot * ch, ch),
                send_sem=send_sem.at[sem], recv_sem=recv_sem.at[sem],
                device_id={"ctx": to}, device_id_type=MESH,
            ).start()

    def send_out(src, dst, sem, first=0, last=blocks):
        if first == 0:
            pltpu.make_async_copy(rows(src, my_slot * ch, ch), rows(dst, q * ch, ch), recv_sem.at[sem]).start()

        for k in range(max(first, 1), last):
            to = peer(k)
            slot = lax.rem(to, 2) * half + lax.div(to, 2)
            pltpu.make_async_remote_copy(
                src_ref=rows(src, slot * ch, ch), dst_ref=rows(dst, q * ch, ch),
                send_sem=send_sem.at[sem], recv_sem=recv_sem.at[sem],
                device_id={"ctx": to}, device_id_type=MESH,
            ).start()

    def pair_copy(src, dst, sem):
        return pltpu.make_async_remote_copy(
            src_ref=src, dst_ref=dst, send_sem=send_sem.at[sem], recv_sem=recv_sem.at[sem],
            device_id={"dp": 1 - d}, device_id_type=MESH,
        )

    H, V, G, HP, CO, GV, GP, GF, GFP = range(9)

    loads[0].wait()

    @pl.when(core == d)
    def _():
        transpose_in(lambda s: in_f[:, s].astype(F32), s_h)

    pl.semaphore_wait(barrier, blocks)

    @pl.when(core == d)
    def _():
        send_in(s_h, r_h, H)

    loads[1].wait()
    transpose_in(lambda s: in_v[:, s].astype(F32), s_v)
    send_in(s_v, r_v, V)
    loads[2].wait()
    loads[3].wait()
    transpose_in(lambda s: (in_gy[:, s].astype(F32) * in_gate[:, s].astype(F32)).astype(BF16).astype(F32), s_g)
    for load in loads[4:]:
        load.wait()

    def tw_at(i):
        return tw[:, i * LANES:(i + 1) * LANES]

    def two_dots(left, table):
        return jnp.dot(left, table[...], preferred_element_type=F32)

    def forward(src, spec):
        x32[...] = src[...].astype(F32)
        for g in range(0, ch, GROUP):
            x = jnp.concatenate(
                [x32[pl.ds(c, blocks, stride=ch), :].astype(BF16) for c in range(g, g + GROUP)], axis=1
            )
            a = jnp.dot(d1[...], jnp.concatenate([x, x], axis=0), preferred_element_type=F32)
            turned = []
            for c in range(GROUP):
                re = a[:blocks, c * LANES:(c + 1) * LANES]
                im = a[blocks:, c * LANES:(c + 1) * LANES]
                turned.append(
                    jnp.concatenate(
                        [
                            (re * tw_at(0) + im * tw_at(1)).astype(BF16),
                            (im * tw_at(0) - re * tw_at(1)).astype(BF16),
                        ],
                        axis=1,
                    )
                )
            spec[g * blocks:(g + GROUP) * blocks, :] = two_dots(jnp.concatenate(turned, axis=0), fwd)

    def inverse(left, right, sign, dst):
        for g in range(0, ch, GROUP):
            part = slice(g * blocks, (g + GROUP) * blocks)
            lr, li = left[part, :LANES], left[part, LANES:]
            rr, ri = right[part, :LANES], right[part, LANES:]
            if sign > 0:
                pr, pi = lr * rr - li * ri, lr * ri + li * rr
            else:
                pr, pi = lr * rr + li * ri, li * rr - lr * ri
            prod = jnp.concatenate([pr.astype(BF16), pi.astype(BF16)], axis=1)
            b = two_dots(prod, inv)
            turned = []
            for c in range(GROUP):
                re = b[c * blocks:(c + 1) * blocks, :LANES]
                im = b[c * blocks:(c + 1) * blocks, LANES:]
                turned.append(
                    jnp.concatenate(
                        [
                            (re * tw_at(2) - im * tw_at(3)).astype(BF16),
                            (im * tw_at(2) + re * tw_at(3)).astype(BF16),
                        ],
                        axis=0,
                    )
                )
            both = jnp.concatenate(turned, axis=1)
            y = jnp.dot(d4[...], jnp.concatenate([both, both], axis=0), preferred_element_type=F32)
            for c in range(GROUP):
                y32[pl.ds(g + c, blocks, stride=ch), :] = y[:, c * LANES:(c + 1) * LANES]
        dst[...] = y32[...].astype(BF16)

    straight = rows(r_h, d * rows_half, rows_half)
    wait_bytes(straight, recv_sem.at[H])
    filter_pass = pair_copy(straight, straight, HP)
    filter_pass.start()
    send_in(s_g, r_g, G)
    wait_bytes(r_v, recv_sem.at[V])
    forward(r_v, spec_v)
    filter_pass.wait()
    forward(r_h, spec_h)
    inverse(spec_v, spec_h, 1, s_c)
    send_out(s_c, r_c, CO)

    wait_bytes(r_g, recv_sem.at[G])
    forward(r_g, spec_g)
    inverse(spec_g, spec_v, -1, s_gf)
    mine = rows(s_gf, d * rows_half, rows_half)
    grad_pass = pair_copy(rows(s_gf, (1 - d) * rows_half, rows_half), r_pair, GP)
    grad_pass.start()
    inverse(spec_g, spec_h, -1, s_gv)
    send_out(s_gv, r_gv, GV, 0, half)
    grad_pass.wait()
    at = pl.ds(pl.multiple_of(d * rows_half, 16), rows_half)
    s_gf[at, :] = (s_gf[at, :].astype(F32) + r_pair[...].astype(F32)).astype(BF16)

    odd = lax.rem(core + d, 2)

    def send_grad(k):
        to = peer(k, odd)
        pltpu.make_async_remote_copy(
            src_ref=rows(s_gf, (d * half + lax.div(to, 2)) * ch, ch), dst_ref=rows(r_gf, q * ch, ch),
            send_sem=send_sem.at[GF], recv_sem=recv_sem.at[GF],
            device_id={"ctx": to}, device_id_type=MESH,
        ).start()

    for k in range(2, blocks, 2):
        send_grad(k)

    @pl.when(core == d)
    def _():
        pltpu.make_async_copy(rows(s_gf, my_slot * ch, ch), rows(r_gf, q * ch, ch), recv_sem.at[GF]).start()

    @pl.when(core != d)
    def _():
        send_grad(0)

    send_out(s_gv, r_gv, GV, half, blocks)

    wait_bytes(r_c, recv_sem.at[CO])
    for j in range(chans // LANES):
        s = slice(j * LANES, (j + 1) * LANES)
        o_gg[0, :, s] = (in_gy[:, s].astype(F32) * r_c[s, :].astype(F32).T).astype(BF16)


    def give_gf():
        for j in range(chans // LANES):
            s = slice(j * LANES, (j + 1) * LANES)
            o_gf[:, s] = r_gf[s, :].astype(F32).T

    @pl.when(core == d)
    def _():
        wait_bytes(r_gf, recv_sem.at[GF])
        pair_copy(r_gf, r_gf, GF).start()
        give_gf()

    wait_bytes(r_gv, recv_sem.at[GV])
    for j in range(chans // LANES):
        s = slice(j * LANES, (j + 1) * LANES)
        o_gv[0, :, s] = r_gv[s, :].astype(F32).T.astype(BF16)

    @pl.when(core != d)
    def _():
        wait_bytes(r_gf, recv_sem.at[GF])
        give_gf()

    most = (blocks - 1) * ch

    @pl.when(core == d)
    def _():
        wait_bytes(s_h.at[pl.ds(0, most), :], send_sem.at[H])
        wait_bytes(s_gf.at[pl.ds(0, rows_half - ch), :], send_sem.at[GF])
        wait_bytes(r_gf, send_sem.at[GF])

    @pl.when(core != d)
    def _():
        wait_bytes(s_gf.at[pl.ds(0, rows_half), :], send_sem.at[GF])

    for ref, sem in ((s_v, V), (s_g, G), (s_c, CO), (s_gv, GV)):
        wait_bytes(ref.at[pl.ds(0, most), :], send_sem.at[sem])


def copy_kernel(*refs):
    count = len(refs) // 2
    sems = refs[-1]
    copies = [pltpu.make_async_copy(refs[i], refs[count + i], sems.at[i]) for i in range(count)]
    for copy in copies:
        copy.start()
    for copy in copies:
        copy.wait()


def body(values, gate_input, filter_param, grad_y, *tables):
    blocks = lax.axis_size("ctx")
    width, chans = filter_param.shape
    vm = lambda shape, kind: pltpu.VMEM(shape, kind)
    block = (width, chans)
    tiles = (chans, width)
    spec = (chans, 2 * width)
    any_spec = pl.BlockSpec(memory_space=pl.ANY)
    out_shape = (
        jax.ShapeDtypeStruct((1, width, chans), BF16),
        jax.ShapeDtypeStruct((1, width, chans), BF16),
        jax.ShapeDtypeStruct((width, chans), F32),
    )
    operands = [pltpu.with_memory_space_constraint(x, pltpu.HBM) for x in (values, gate_input, filter_param, grad_y, *tables)]
    results = pl.pallas_call(
        functools.partial(kernel, blocks),
        out_shape=out_shape,
        in_specs=[any_spec] * 9,
        out_specs=(pl.BlockSpec(memory_space=pltpu.VMEM),) * 3,
        scratch_shapes=[vm(block, BF16)] * 4
        + [vm(t.shape, t.dtype) for t in tables]
        + [vm(tiles, BF16)] * 6
        + [vm(tiles, F32)] * 2
        + [vm(spec, F32)] * 3
        + [vm(tiles, BF16)] * 3
        + [vm((chans // 2, width), BF16)]
        + [vm(tiles, BF16)] * 3
        + [
            pltpu.SemaphoreType.DMA((9,)),
            pltpu.SemaphoreType.DMA((9,)),
            pltpu.SemaphoreType.DMA((9,)),
        ],
        compiler_params=pltpu.CompilerParams(
            collective_id=0, has_side_effects=True, vmem_limit_bytes=40 * 1024 * 1024
        ),
        cost_estimate=pl.CostEstimate(flops=1_000_000_000, bytes_accessed=4_000_000, transcendentals=0),
    )(*operands)
    return pl.pallas_call(
        copy_kernel,
        out_shape=out_shape,
        in_specs=[any_spec] * 3,
        out_specs=(any_spec,) * 3,
        scratch_shapes=[pltpu.SemaphoreType.DMA((3,))],
        compiler_params=pltpu.CompilerParams(vmem_limit_bytes=4 * 1024 * 1024),
    )(*results)


def solution(mesh):
    blocks = mesh.shape["ctx"]
    tables = make_tables(blocks, LANES)
    placed = (P("dp", "ctx", "tp"), P("dp", "ctx", "tp"), P("ctx", "tp"), P("dp", "ctx", "tp"))
    mapped = jax.shard_map(
        body,
        mesh=mesh,
        in_specs=placed + (P(),) * len(tables),
        out_specs=(P("dp", "ctx", "tp"), P("dp", "ctx", "tp"), P("ctx", "tp")),
        check_vma=False,
    )

    def run(values, gate_input, filter_param, grad_y):
        return mapped(values, gate_input, filter_param, grad_y, *tables)

    return run
```

```python
import functools
import math

import jax
import jax.numpy as jnp
import ml_dtypes
import numpy as np
from jax import lax
from jax.experimental import pallas as pl
from jax.experimental.pallas import tpu as pltpu
from jax.sharding import PartitionSpec as P

MESH = pl.DeviceIdType.MESH
F32 = jnp.float32
BF16 = jnp.bfloat16
LANES = 128
GROUP = 8


def make_tables(blocks, width):
    length = blocks * width
    half = blocks // 2
    block_of = np.concatenate([np.arange(half) * 2, np.arange(half) * 2 + 1]).astype(np.float64)
    k1 = np.arange(blocks, dtype=np.float64) + 0.25
    n2 = np.arange(width, dtype=np.float64)
    ang1 = 2.0 * np.pi * k1[:, None] * block_of[None, :] / blocks
    d1 = np.concatenate([np.cos(ang1), -np.sin(ang1)], axis=0)
    d4 = np.concatenate([np.cos(ang1), -np.sin(ang1)], axis=0).T
    ang2 = 2.0 * np.pi * k1[:, None] * n2[None, :] / length
    tw = np.concatenate([np.cos(ang2), np.sin(ang2)], axis=1)
    scale = 1.0 / (length * math.sqrt(length))
    ang3 = 2.0 * np.pi * n2[:, None] * n2[None, :] / width
    co, si = np.cos(ang3), np.sin(ang3)
    fwd = np.block([[co, -si], [si, co]])
    inv = np.block([[co, si], [-si, co]])

    def two_parts(table, axis):
        high = np.asarray(table, ml_dtypes.bfloat16)
        low = np.asarray(table - high.astype(np.float64), ml_dtypes.bfloat16)
        return jnp.asarray(np.concatenate([high, low], axis=axis))

    return (
        two_parts(d1, 1),
        two_parts(d4, 1),
        jnp.asarray(np.concatenate([tw, tw * scale], axis=1), F32),
        jnp.asarray(fwd, BF16),
        jnp.asarray(inv, BF16),
    )


def kernel(
    blocks,
    v_hbm, gate_hbm, f_hbm, gy_hbm, d1_hbm, d4_hbm, tw_hbm, fwd_hbm, inv_hbm,
    o_gg, o_gv, o_gf,
    in_v, in_gate, in_f, in_gy, d1, d4, tw, fwd, inv,
    s_h, s_v, s_g, r_h, r_v, r_g,
    x32, y32, spec_h, spec_v, spec_g,
    s_c, s_gv, s_gf, r_pair, r_c, r_gv, r_gf,
    in_sem, send_sem, recv_sem,
):
    chans = in_v.shape[1]
    width = in_v.shape[0]
    ch = chans // blocks
    half = blocks // 2
    rows_half = half * ch
    d = lax.axis_index("dp")
    q = lax.axis_index("ctx")
    core = q % 2
    my_z, my_e = q // 4, q % 4
    zs = blocks // 4
    my_slot = core * half + q // 2

    loads = [
        pltpu.make_async_copy(src, dst, in_sem.at[i])
        for i, (src, dst) in enumerate(
            [
                (f_hbm, in_f), (v_hbm.at[0], in_v), (gy_hbm.at[0], in_gy), (gate_hbm.at[0], in_gate),
                (d1_hbm, d1), (tw_hbm, tw), (fwd_hbm, fwd), (inv_hbm, inv), (d4_hbm, d4),
            ]
        )
    ]
    loads[0].start()

    def peer(k, turned=0):
        step, e = k // 4, k % 4
        turn = step // 2
        dist = (turn + 1) // 2
        dz = (zs - dist if turn % 2 else dist) + step % 2 * (zs // 2)
        return lax.rem(my_z + dz, zs) * 4 + lax.rem(my_e + e + turned, 4)

    barrier = pltpu.get_barrier_semaphore()

    for k in range(1, blocks):
        pl.semaphore_signal(barrier, inc=1, device_id={"ctx": peer(k)}, device_id_type=MESH)
    pl.semaphore_signal(barrier, inc=1, device_id={"dp": 1 - d}, device_id_type=MESH)
    for load in loads[1:]:
        load.start()

    def rows(ref, start, count):
        return ref.at[pl.ds(pl.multiple_of(start, 16), count), :]

    def wait_bytes(ref, sem):
        pltpu.make_async_copy(ref, ref, sem).wait()

    def transpose_in(block_of, dst):
        for j in range(chans // LANES):
            dst[j * LANES:(j + 1) * LANES, :] = block_of(slice(j * LANES, (j + 1) * LANES)).T.astype(BF16)

    def send_in(src, dst, sem):
        pltpu.make_async_copy(rows(src, q * ch, ch), rows(dst, my_slot * ch, ch), recv_sem.at[sem]).start()

        for k in range(1, blocks):
            to = peer(k)
            pltpu.make_async_remote_copy(
                src_ref=rows(src, to * ch, ch), dst_ref=rows(dst, my_slot * ch, ch),
                send_sem=send_sem.at[sem], recv_sem=recv_sem.at[sem],
                device_id={"ctx": to}, device_id_type=MESH,
            ).start()

    def send_out(src, dst, sem, first=0, last=blocks):
        if first == 0:
            pltpu.make_async_copy(rows(src, my_slot * ch, ch), rows(dst, q * ch, ch), recv_sem.at[sem]).start()

        for k in range(max(first, 1), last):
            to = peer(k)
            slot = lax.rem(to, 2) * half + lax.div(to, 2)
            pltpu.make_async_remote_copy(
                src_ref=rows(src, slot * ch, ch), dst_ref=rows(dst, q * ch, ch),
                send_sem=send_sem.at[sem], recv_sem=recv_sem.at[sem],
                device_id={"ctx": to}, device_id_type=MESH,
            ).start()

    def pair_copy(src, dst, sem):
        return pltpu.make_async_remote_copy(
            src_ref=src, dst_ref=dst, send_sem=send_sem.at[sem], recv_sem=recv_sem.at[sem],
            device_id={"dp": 1 - d}, device_id_type=MESH,
        )

    H, V, G, HP, CO, GV, GP, GF, GFP = range(9)

    loads[0].wait()

    @pl.when(core == d)
    def _():
        transpose_in(lambda s: in_f[:, s].astype(F32), s_h)

    pl.semaphore_wait(barrier, blocks)

    @pl.when(core == d)
    def _():
        send_in(s_h, r_h, H)

    loads[1].wait()
    transpose_in(lambda s: in_v[:, s].astype(F32), s_v)
    send_in(s_v, r_v, V)
    loads[2].wait()
    loads[3].wait()
    transpose_in(lambda s: (in_gy[:, s].astype(F32) * in_gate[:, s].astype(F32)).astype(BF16).astype(F32), s_g)
    for load in loads[4:]:
        load.wait()

    def tw_at(i):
        return tw[:, i * LANES:(i + 1) * LANES]

    def two_dots(left, table):
        return jnp.dot(left, table[...], preferred_element_type=F32)

    def forward(src, spec):
        x32[...] = src[...].astype(F32)
        for g in range(0, ch, GROUP):
            x = jnp.concatenate(
                [x32[pl.ds(c, blocks, stride=ch), :].astype(BF16) for c in range(g, g + GROUP)], axis=1
            )
            a = jnp.dot(d1[...], jnp.concatenate([x, x], axis=0), preferred_element_type=F32)
            turned = []
            for c in range(GROUP):
                re = a[:blocks, c * LANES:(c + 1) * LANES]
                im = a[blocks:, c * LANES:(c + 1) * LANES]
                turned.append(
                    jnp.concatenate(
                        [
                            (re * tw_at(0) + im * tw_at(1)).astype(BF16),
                            (im * tw_at(0) - re * tw_at(1)).astype(BF16),
                        ],
                        axis=1,
                    )
                )
            spec[g * blocks:(g + GROUP) * blocks, :] = two_dots(jnp.concatenate(turned, axis=0), fwd)

    def inverse(left, right, sign, dst):
        for g in range(0, ch, GROUP):
            part = slice(g * blocks, (g + GROUP) * blocks)
            lr, li = left[part, :LANES], left[part, LANES:]
            rr, ri = right[part, :LANES], right[part, LANES:]
            if sign > 0:
                pr, pi = lr * rr - li * ri, lr * ri + li * rr
            else:
                pr, pi = lr * rr + li * ri, li * rr - lr * ri
            prod = jnp.concatenate([pr.astype(BF16), pi.astype(BF16)], axis=1)
            b = two_dots(prod, inv)
            turned = []
            for c in range(GROUP):
                re = b[c * blocks:(c + 1) * blocks, :LANES]
                im = b[c * blocks:(c + 1) * blocks, LANES:]
                turned.append(
                    jnp.concatenate(
                        [
                            (re * tw_at(2) - im * tw_at(3)).astype(BF16),
                            (im * tw_at(2) + re * tw_at(3)).astype(BF16),
                        ],
                        axis=0,
                    )
                )
            both = jnp.concatenate(turned, axis=1)
            y = jnp.dot(d4[...], jnp.concatenate([both, both], axis=0), preferred_element_type=F32)
            for c in range(GROUP):
                y32[pl.ds(g + c, blocks, stride=ch), :] = y[:, c * LANES:(c + 1) * LANES]
        dst[...] = y32[...].astype(BF16)

    straight = rows(r_h, d * rows_half, rows_half)
    wait_bytes(straight, recv_sem.at[H])
    filter_pass = pair_copy(straight, straight, HP)
    filter_pass.start()
    send_in(s_g, r_g, G)
    wait_bytes(r_v, recv_sem.at[V])
    forward(r_v, spec_v)
    filter_pass.wait()
    forward(r_h, spec_h)
    inverse(spec_v, spec_h, 1, s_c)
    send_out(s_c, r_c, CO)

    wait_bytes(r_g, recv_sem.at[G])
    forward(r_g, spec_g)
    inverse(spec_g, spec_v, -1, s_gf)
    mine = rows(s_gf, d * rows_half, rows_half)
    grad_pass = pair_copy(rows(s_gf, (1 - d) * rows_half, rows_half), r_pair, GP)
    grad_pass.start()
    inverse(spec_g, spec_h, -1, s_gv)
    send_out(s_gv, r_gv, GV, 0, half)
    grad_pass.wait()
    at = pl.ds(pl.multiple_of(d * rows_half, 16), rows_half)
    s_gf[at, :] = (s_gf[at, :].astype(F32) + r_pair[...].astype(F32)).astype(BF16)

    odd = lax.rem(core + d, 2)

    def send_grad(k):
        to = peer(k, odd)
        pltpu.make_async_remote_copy(
            src_ref=rows(s_gf, (d * half + lax.div(to, 2)) * ch, ch), dst_ref=rows(r_gf, q * ch, ch),
            send_sem=send_sem.at[GF], recv_sem=recv_sem.at[GF],
            device_id={"ctx": to}, device_id_type=MESH,
        ).start()

    for k in range(2, blocks, 2):
        send_grad(k)

    @pl.when(core == d)
    def _():
        pltpu.make_async_copy(rows(s_gf, my_slot * ch, ch), rows(r_gf, q * ch, ch), recv_sem.at[GF]).start()

    @pl.when(core != d)
    def _():
        send_grad(0)

    send_out(s_gv, r_gv, GV, half, blocks)

    wait_bytes(r_c, recv_sem.at[CO])
    for j in range(chans // LANES):
        s = slice(j * LANES, (j + 1) * LANES)
        o_gg[0, :, s] = (in_gy[:, s].astype(F32) * r_c[s, :].astype(F32).T).astype(BF16)


    def give_gf():
        for j in range(chans // LANES):
            s = slice(j * LANES, (j + 1) * LANES)
            o_gf[:, s] = r_gf[s, :].astype(F32).T

    @pl.when(core == d)
    def _():
        wait_bytes(r_gf, recv_sem.at[GF])
        pair_copy(r_gf, r_gf, GF).start()
        give_gf()

    wait_bytes(r_gv, recv_sem.at[GV])
    for j in range(chans // LANES):
        s = slice(j * LANES, (j + 1) * LANES)
        o_gv[0, :, s] = r_gv[s, :].astype(F32).T.astype(BF16)

    @pl.when(core != d)
    def _():
        wait_bytes(r_gf, recv_sem.at[GF])
        give_gf()

    most = (blocks - 1) * ch

    @pl.when(core == d)
    def _():
        wait_bytes(s_h.at[pl.ds(0, most), :], send_sem.at[H])
        wait_bytes(s_gf.at[pl.ds(0, rows_half - ch), :], send_sem.at[GF])
        wait_bytes(r_gf, send_sem.at[GF])

    @pl.when(core != d)
    def _():
        wait_bytes(s_gf.at[pl.ds(0, rows_half), :], send_sem.at[GF])

    for ref, sem in ((s_v, V), (s_g, G), (s_c, CO), (s_gv, GV)):
        wait_bytes(ref.at[pl.ds(0, most), :], send_sem.at[sem])


def copy_kernel(*refs):
    count = len(refs) // 2
    sems = refs[-1]
    copies = [pltpu.make_async_copy(refs[i], refs[count + i], sems.at[i]) for i in range(count)]
    for copy in copies:
        copy.start()
    for copy in copies:
        copy.wait()


def body(values, gate_input, filter_param, grad_y, *tables):
    blocks = lax.axis_size("ctx")
    width, chans = filter_param.shape
    vm = lambda shape, kind: pltpu.VMEM(shape, kind)
    block = (width, chans)
    tiles = (chans, width)
    spec = (chans, 2 * width)
    any_spec = pl.BlockSpec(memory_space=pl.ANY)
    out_shape = (
        jax.ShapeDtypeStruct((1, width, chans), BF16),
        jax.ShapeDtypeStruct((1, width, chans), BF16),
        jax.ShapeDtypeStruct((width, chans), F32),
    )
    operands = [pltpu.with_memory_space_constraint(x, pltpu.HBM) for x in (values, gate_input, filter_param, grad_y, *tables)]
    results = pl.pallas_call(
        functools.partial(kernel, blocks),
        out_shape=out_shape,
        in_specs=[any_spec] * 9,
        out_specs=(pl.BlockSpec(memory_space=pltpu.VMEM),) * 3,
        scratch_shapes=[vm(block, BF16)] * 4
        + [vm(t.shape, t.dtype) for t in tables]
        + [vm(tiles, BF16)] * 6
        + [vm(tiles, F32)] * 2
        + [vm(spec, F32)] * 3
        + [vm(tiles, BF16)] * 3
        + [vm((chans // 2, width), BF16)]
        + [vm(tiles, BF16)] * 3
        + [
            pltpu.SemaphoreType.DMA((9,)),
            pltpu.SemaphoreType.DMA((9,)),
            pltpu.SemaphoreType.DMA((9,)),
        ],
        compiler_params=pltpu.CompilerParams(
            collective_id=0, has_side_effects=True, vmem_limit_bytes=40 * 1024 * 1024
        ),
        cost_estimate=pl.CostEstimate(flops=1_000_000_000, bytes_accessed=4_000_000, transcendentals=0),
    )(*operands)
    return pl.pallas_call(
        copy_kernel,
        out_shape=out_shape,
        in_specs=[any_spec] * 3,
        out_specs=(any_spec,) * 3,
        scratch_shapes=[pltpu.SemaphoreType.DMA((3,))],
        compiler_params=pltpu.CompilerParams(vmem_limit_bytes=4 * 1024 * 1024),
    )(*results)


def solution(mesh):
    blocks = mesh.shape["ctx"]
    tables = make_tables(blocks, LANES)
    placed = (P("dp", "ctx", "tp"), P("dp", "ctx", "tp"), P("ctx", "tp"), P("dp", "ctx", "tp"))
    mapped = jax.shard_map(
        body,
        mesh=mesh,
        in_specs=placed + (P(),) * len(tables),
        out_specs=(P("dp", "ctx", "tp"), P("dp", "ctx", "tp"), P("ctx", "tp")),
        check_vma=False,
    )

    def run(values, gate_input, filter_param, grad_y):
        return mapped(values, gate_input, filter_param, grad_y, *tables)

    return run
```
